256 devices in a mesh: dp: 32 (over x, y, core), tensor: 8 (over z).
Axes of the slice: x: 4, y: 4, z: 8, core: 2. Of those that a mesh axis runs over, the one named last changes fastest.
Arguments:
- gradients: bfloat16 [32, 2, 320, 14336], P('dp', None, None, 'tensor'), may hold values from -6 to 6
- feedback: float32 [32, 2, 320, 14336], P('dp', None, None, 'tensor'), may hold values from -4 to 4
- seed_value: int32 [1], replicated, may hold values from 0 to 29999
Outputs:
- new_feedback: float32 [32, 2, 320, 14336], P('dp', None, None, 'tensor')
- left_basis: float32 [2, 320, 128], replicated
- right_factor: float32 [2, 14336, 128], P(None, 'tensor')
The draws below stay inside these ranges and needn't reach their ends.
All inputs are finite; a program needn't handle non-finite values.
Results may differ from the reference program's by a relative error of at most 0.0003.
Values sent between devices are 32-bit elements; how exact they have to be, the bound alone decides.
No kernel may reach another device: no remote copies, remote signals or barrier semaphores. Data moves between devices by JAX's collectives and lax.ppermute only.
A program may use at most 64 MiB of HBM per device.

```python
import jax
import jax.numpy as jnp
from jax import lax

MATS = 2
ROWS = 320
FF = 14336
RANK = 128
REPLICAS = 32
N_DP = 32


def shard_levels(stream_key, shape, cuts, least, largest):
    def one(position, parts):
        heights = jax.random.uniform(jax.random.fold_in(jax.random.fold_in(stream_key, 6), position), (parts,), jnp.float32, least / len(cuts), largest / len(cuts))
        return jnp.repeat(jnp.exp(heights), shape[position] // parts).reshape((-1,) + (1,) * (len(shape) - position - 1))

    level = one(*cuts[0])
    for cut in cuts[1:]:
        level = level * one(*cut)
    return level


def bell_draw(rng, dims, width, reach, pieces=(), kind=jnp.bfloat16):
    values = width * jax.random.normal(rng, dims, jnp.float32)
    if pieces:
        values = values * shard_levels(rng, dims, pieces, -0.22, 0.18)
    return jnp.clip(values, -reach, reach).astype(kind)


def setup_inputs(seed: int = 0) -> dict:
    keys = jax.random.split(jax.random.key(seed), 4)
    gradients = bell_draw(keys[0], (REPLICAS, MATS, ROWS, FF), 1.0, 6.0, ((0, 32), (3, 8)))
    feedback = bell_draw(keys[1], (REPLICAS, MATS, ROWS, FF), 0.5, 4.0, ((0, 32), (3, 8)), jnp.float32)
    seed_value = jax.random.randint(keys[2], (1,), 0, 30000).astype(jnp.int32)
    return {"gradients": gradients, "feedback": feedback, "seed_value": seed_value}


unit_scale = 3.4641016

def start_factor(seed_scalar, col_start, columns, rank_count):
    col_ids = col_start + jnp.arange(columns, dtype=jnp.int32)[:, None]
    rank_ids = jnp.arange(rank_count, dtype=jnp.int32)[None, :]
    hashed = (col_ids * 131 + rank_ids * 977 + seed_scalar) % 32749
    hashed = (hashed * hashed + rank_ids * 17 + 7) % 32749
    hashed = (hashed * hashed + col_ids) % 32749
    return (hashed.astype(jnp.float32) / 32749.0 - 0.5) * unit_scale

def reference(gradients, feedback, seed_value):
    highest = lax.Precision.HIGHEST
    start_right = start_factor(seed_value[0].astype(jnp.int32), 0, FF, RANK)
    summed_in = gradients.astype(jnp.float32) + feedback
    averaged = jnp.sum(summed_in, axis=0) / N_DP
    left_sum = jnp.einsum('mrc,ck->mrk', averaged, start_right, precision=highest)
    gram_sums = jnp.einsum('mrk,mrj->mkj', left_sum, left_sum, precision=highest)
    factor_low = jnp.linalg.cholesky(gram_sums)
    left_basis = lax.linalg.triangular_solve(factor_low, left_sum, left_side=False, lower=True, transpose_a=True)
    right_factor = jnp.einsum('mrc,mrk->mck', averaged, left_basis, precision=highest)
    rebuilt = jnp.einsum('mrk,mck->mrc', left_basis, right_factor, precision=highest)
    new_feedback = summed_in - rebuilt[None]
    return (new_feedback, left_basis, right_factor)
```

```python
import functools

import jax
import jax.numpy as jnp
from jax import lax
from jax.experimental import pallas as pl
from jax.experimental.pallas import tpu as pltpu
from jax.sharding import Mesh, PartitionSpec as P

RANK = 128
PRIME = 32749
SIDE = 4
CORES = 2
CHUNK = 256

unit_scale = 3.4641016
f32 = jnp.float32
bf16 = jnp.bfloat16


def split(x):
    high = x.astype(bf16)
    return high, (x - high.astype(f32)).astype(bf16)


def dot(a, b, contract=((1,), (0,))):
    return lax.dot_general(a, b, (contract, ((), ())), preferred_element_type=f32)


def exact_dot(a, b, contract):
    return lax.dot_general(
        a, b, (contract, ((), ())), precision=lax.Precision.HIGHEST, preferred_element_type=f32
    )


def modulo(x):
    quotient = (x.astype(f32) * (0.999999 / PRIME)).astype(jnp.int32)
    rest = x - quotient * PRIME
    return jnp.where(rest >= PRIME, rest - PRIME, rest)


def start_block(seed, first, columns):
    col = first + lax.broadcasted_iota(jnp.int32, (columns, RANK), 0)
    rank = lax.broadcasted_iota(jnp.int32, (columns, RANK), 1)
    hashed = modulo(col * 131 + rank * 977 + seed)
    hashed = modulo(hashed * hashed + rank * 17 + 7)
    hashed = modulo(hashed * hashed + col)
    return (hashed.astype(f32) * (1.0 / PRIME) - 0.5) * unit_scale


def left_kernel(where_ref, grad_ref, feed_ref, out_ref):
    step = pl.program_id(0)
    seed, first, core = where_ref[0], where_ref[1], where_ref[2]
    start = start_block(seed, first + step * CHUNK, CHUNK)
    high, low = split(start)
    both = jnp.concatenate([high, low], axis=1)
    for m in range(2):
        s_high, s_low = split(grad_ref[m].astype(f32) + feed_ref[m])
        wide = dot(s_high, both)
        part = wide[:, :RANK] + wide[:, RANK:] + dot(s_low, high)
        slot = m ^ core

        @pl.when(step == 0)
        def _():
            out_ref[slot] = part

        @pl.when(step > 0)
        def _():
            out_ref[slot] += part


def basis_kernel(left_ref, basis_ref):
    left = left_ref[...] * (1.0 / 32)
    gram = exact_dot(left, left, ((0,), (0,)))
    lane = lax.broadcasted_iota(jnp.int32, (1, RANK), 1)
    rows8 = lax.broadcasted_iota(jnp.int32, (8, RANK), 0)
    blocks = [gram[8 * b : 8 * b + 8, :] for b in range(RANK // 8)]
    pivots = []
    for j in range(RANK):
        at = lane == j
        bj, sj = j // 8, j % 8
        row = blocks[bj][sj : sj + 1, :]
        pivot = jnp.broadcast_to(row[:, j : j + 1], (1, RANK))
        pivots.append(pivot)
        inverse = 1.0 / pivot
        row = jnp.where(at, 1.0, row)
        for b in range(bj, RANK // 8):
            block = blocks[b]
            factor = jnp.broadcast_to(block[:, j : j + 1], (8, RANK)) * inverse
            kept = jnp.where(at, 0.0, block)
            if b == bj:
                if sj == 7:
                    continue
                blocks[b] = jnp.where(rows8 > sj, kept - factor * row, block)
            else:
                blocks[b] = kept - factor * row
    lower = jnp.concatenate(blocks, axis=0)
    i = lax.broadcasted_iota(jnp.int32, (RANK, RANK), 0)
    j = lax.broadcasted_iota(jnp.int32, (RANK, RANK), 1)
    scale = lax.rsqrt(jnp.concatenate(pivots, axis=0))
    inverse = jnp.where(i > j, lower, jnp.where(i == j, 1.0, 0.0)) * scale
    basis_ref[...] = exact_dot(left, inverse, ((1,), (1,)))


def right_kernel(where_ref, mine_ref, other_ref, grad_ref, feed_ref, out_ref, basis_ref, wide_ref):
    core = where_ref[2]

    @pl.when(pl.program_id(0) == 0)
    def _():
        for m in range(2):
            basis = jnp.where(core == m, mine_ref[...], other_ref[...])
            basis_ref[m] = basis
            flipped = basis.T
            high, low = split(flipped)
            wide_ref[m, :RANK, :] = high
            wide_ref[m, RANK:, :] = low

    for m in range(2):
        s_high, s_low = split(grad_ref[m].astype(f32) + feed_ref[m])
        wide = dot(wide_ref[m], s_high)
        part = wide[:RANK] + wide[RANK:] + dot(wide_ref[m, :RANK, :], s_low)
        out_ref[m ^ core] = part


def update_kernel(where_ref, basis_ref, mine_ref, other_ref, grad_ref, feed_ref, out_ref, right_ref, wide_ref):
    core = where_ref[2]

    @pl.when(pl.program_id(0) == 0)
    def _():
        for m in range(2):
            high, low = split(basis_ref[m])
            wide_ref[m, :, :RANK] = high
            wide_ref[m, :, RANK:] = low

    for m in range(2):
        right = jnp.where(core == m, mine_ref[...], other_ref[...])
        right_ref[m] = right.T
        high, low = split(right)
        rebuilt = dot(wide_ref[m], jnp.concatenate([high, high], axis=0)) + dot(wide_ref[m, :, :RANK], low)
        out_ref[m] = grad_ref[m].astype(f32) + feed_ref[m] - rebuilt


def params(**more):
    return pltpu.CompilerParams(dimension_semantics=("arbitrary",), vmem_limit_bytes=40 * 1024 * 1024)


def whole(*shape):
    return pl.BlockSpec(shape, lambda i: (0,) * len(shape))


def spread(x, axes, count):
    return lax.all_to_all(jnp.broadcast_to(x[None], (count,) + x.shape), axes, 0, 0)


def swap(x):
    return lax.ppermute(x, "core", [(0, 1), (1, 0)])


def on_device(gradients, feedback, seed_value):
    gradients, feedback = gradients[0], feedback[0]
    mats, rows, columns = gradients.shape
    chips = SIDE * SIDE
    depth = lax.axis_size("z")
    core = lax.axis_index("core")
    where = jnp.stack([seed_value[0], lax.axis_index("z") * columns, core]).astype(jnp.int32)
    steps = columns // CHUNK
    smem = pl.BlockSpec(memory_space=pltpu.SMEM)
    wide_spec = pl.BlockSpec((mats, rows, CHUNK), lambda i: (0, 0, i))

    left_part = pl.pallas_call(
        left_kernel,
        grid=(steps,),
        in_specs=[smem, wide_spec, wide_spec],
        out_specs=whole(mats, rows, RANK),
        out_shape=jax.ShapeDtypeStruct((mats, rows, RANK), f32),
        compiler_params=params(),
        name="left_part",
    )(where, gradients, feedback)

    left = left_part[0] + swap(left_part[1])
    left = lax.all_to_all(left.reshape(chips, rows // chips, RANK), ("x", "y"), 0, 0).sum(0)
    left = spread(left, "z", depth).sum(0)
    left = spread(left, ("x", "y"), chips).reshape(rows, RANK)

    basis_mine = pl.pallas_call(
        basis_kernel,
        out_shape=jax.ShapeDtypeStruct((rows, RANK), f32),
        compiler_params=pltpu.CompilerParams(vmem_limit_bytes=40 * 1024 * 1024),
        name="basis",
    )(left)
    basis_other = swap(basis_mine)

    right_part, left_basis = pl.pallas_call(
        right_kernel,
        grid=(steps,),
        in_specs=[smem, whole(rows, RANK), whole(rows, RANK), wide_spec, wide_spec],
        out_specs=[pl.BlockSpec((mats, RANK, CHUNK), lambda i: (0, 0, i)), whole(mats, rows, RANK)],
        out_shape=[
            jax.ShapeDtypeStruct((mats, RANK, columns), f32),
            jax.ShapeDtypeStruct((mats, rows, RANK), f32),
        ],
        scratch_shapes=[pltpu.VMEM((mats, 2 * RANK, rows), bf16)],
        compiler_params=params(),
        name="right_part",
    )(where, basis_mine, basis_other, gradients, feedback)

    right = right_part[0] + swap(right_part[1])
    right = lax.all_to_all(right.reshape(chips, RANK // chips, columns), ("x", "y"), 0, 0).sum(0) * (1.0 / 32)
    right_mine = spread(right, ("x", "y"), chips).reshape(RANK, columns)
    right_other = swap(right_mine)

    flat_spec = pl.BlockSpec((RANK, CHUNK), lambda i: (0, i))
    new_feedback, right_factor = pl.pallas_call(
        update_kernel,
        grid=(steps,),
        in_specs=[smem, whole(mats, rows, RANK), flat_spec, flat_spec, wide_spec, wide_spec],
        out_specs=[wide_spec, pl.BlockSpec((mats, CHUNK, RANK), lambda i: (0, i, 0))],
        out_shape=[
            jax.ShapeDtypeStruct((mats, rows, columns), f32),
            jax.ShapeDtypeStruct((mats, columns, RANK), f32),
        ],
        scratch_shapes=[pltpu.VMEM((mats, rows, 2 * RANK), bf16)],
        compiler_params=params(),
        name="update",
    )(where, left_basis, right_mine, right_other, gradients, feedback)
    return new_feedback[None], left_basis, right_factor


def solution(mesh):
    fine = Mesh(mesh.devices.reshape(SIDE, SIDE, CORES, -1), ("x", "y", "core", "z"))
    dp = ("x", "y", "core")
    placed = (P(dp, None, None, "z"), P(dp, None, None, "z"), P())
    return jax.shard_map(
        on_device,
        mesh=fine,
        in_specs=placed,
        out_specs=(P(dp, None, None, "z"), P(), P(None, "z", None)),
        check_vma=False,
    )
```

```python
import functools

import jax
import jax.numpy as jnp
from jax import lax
from jax.experimental import pallas as pl
from jax.experimental.pallas import tpu as pltpu
from jax.sharding import Mesh, PartitionSpec as P

RANK = 128
PRIME = 32749
SIDE = 4
CORES = 2
CHUNK = 256
GROUP = 8
MIB = 1024 * 1024

unit_scale = 3.4641016
f32 = jnp.float32
bf16 = jnp.bfloat16

smem = pl.BlockSpec(memory_space=pltpu.SMEM)
hbm = pl.BlockSpec(memory_space=pltpu.HBM)
vmem = pl.BlockSpec(memory_space=pltpu.VMEM)


def split(x):
    high = x.astype(bf16)
    return high, (x - high.astype(f32)).astype(bf16)


def dot(a, b, contract=((1,), (0,))):
    return lax.dot_general(a, b, (contract, ((), ())), preferred_element_type=f32)


def exact_dot(a, b, contract):
    return lax.dot_general(
        a, b, (contract, ((), ())), precision=lax.Precision.HIGHEST, preferred_element_type=f32
    )


def cols(j):
    return pl.ds(j * CHUNK, CHUNK)


def centred(x):
    quotient = (x.astype(f32) * (1.0 / PRIME) + 0.5).astype(jnp.int32)
    return x - quotient * PRIME


def start_block(seed, first, columns):
    col = first + lax.broadcasted_iota(jnp.int32, (columns, RANK), 0)
    rank = lax.broadcasted_iota(jnp.int32, (columns, RANK), 1)
    hashed = centred(col * 131 + rank * 977 + seed)
    hashed = centred(hashed * hashed + rank * 17 + 7)
    hashed = centred(hashed * hashed + col)
    hashed = jnp.where(hashed < 0, hashed + PRIME, hashed)
    return (hashed.astype(f32) * (1.0 / PRIME) - 0.5) * unit_scale


def left_kernel(where_ref, grad_hbm, feed_hbm, out_ref, grad_ref, feed_ref, start_ref, sems):
    seed, first, core = where_ref[0], where_ref[1], where_ref[2]
    steps = grad_ref.shape[2] // CHUNK
    copies = []
    for j in range(steps):
        pair = (
            pltpu.make_async_copy(grad_hbm.at[:, :, cols(j)], grad_ref.at[:, :, cols(j)], sems.at[j, 0]),
            pltpu.make_async_copy(feed_hbm.at[:, :, cols(j)], feed_ref.at[:, :, cols(j)], sems.at[j, 1]),
        )
        for copy in pair:
            copy.start()
        copies.append(pair)
    for j in range(steps):
        high, low = split(start_block(seed, first + j * CHUNK, CHUNK))
        start_ref[cols(j), :RANK] = high
        start_ref[cols(j), RANK:] = low
    for j in range(steps):
        for copy in copies[j]:
            copy.wait()
        both = start_ref[cols(j), :]
        for m in range(2):
            s_high, s_low = split(grad_ref[m, :, cols(j)].astype(f32) + feed_ref[m, :, cols(j)])
            wide = dot(s_high, both)
            part = wide[:, :RANK] + wide[:, RANK:] + dot(s_low, both[:, :RANK])
            if j == 0:
                out_ref[m ^ core] = part
            else:
                out_ref[m ^ core] += part


def eliminate(gram):
    lane = lax.broadcasted_iota(jnp.int32, (1, RANK), 1)
    count = RANK // GROUP
    blocks = [gram[GROUP * b : GROUP * (b + 1), :] for b in range(count)]
    sub = lax.broadcasted_iota(jnp.int32, (GROUP, RANK), 0)
    pivots = []
    for b in range(count):
        start = GROUP * b
        panel = blocks[b]
        spread_cols = [jnp.broadcast_to(panel[:, start + t : start + t + 1], (GROUP, RANK)) for t in range(GROUP)]
        a = [[spread_cols[t][s : s + 1, :] for t in range(GROUP)] for s in range(GROUP)]
        factors = [[None] * GROUP for _ in range(GROUP)]
        inverses = []
        for t in range(GROUP):
            pivots.append(a[t][t])
            inverses.append(1.0 / a[t][t])
            for s in range(t + 1, GROUP):
                factors[s][t] = a[s][t] * inverses[t]
                for u in range(t + 1, GROUP):
                    a[s][u] = a[s][u] - factors[s][t] * a[t][u]
        rows, sources = [], []
        for s in range(GROUP):
            row = panel[s : s + 1, :]
            for t in range(s):
                row = jnp.where(lane == start + t, 0.0, row) - factors[s][t] * sources[t]
            rows.append(row)
            sources.append(jnp.where(lane == start + s, 1.0, row))
        for s in range(GROUP):
            panel = jnp.where(sub == s, rows[s], panel)
        blocks[b] = panel
        for later in range(b + 1, count):
            block = blocks[later]
            heads = [jnp.broadcast_to(block[:, start + t : start + t + 1], (GROUP, RANK)) for t in range(GROUP)]
            for t in range(GROUP):
                factor = heads[t] * inverses[t]
                for u in range(t + 1, GROUP):
                    heads[u] = heads[u] - factor * a[t][u]
                block = jnp.where(lane == start + t, 0.0, block) - factor * sources[t]
            blocks[later] = block
    return jnp.concatenate(blocks, axis=0), jnp.concatenate(pivots, axis=0)


def basis_kernel(left_ref, basis_ref, inverse_ref):
    left = left_ref[...] * (1.0 / 32)
    lower, pivots = eliminate(exact_dot(left, left, ((0,), (0,))))
    i = lax.broadcasted_iota(jnp.int32, (RANK, RANK), 0)
    j = lax.broadcasted_iota(jnp.int32, (RANK, RANK), 1)
    inverse = jnp.where(i > j, lower, jnp.where(i == j, 1.0, 0.0)) * lax.rsqrt(pivots)
    inverse_ref[...] = inverse
    basis_ref[...] = exact_dot(left, inverse, ((1,), (1,)))


def right_kernel(where_ref, mine_ref, other_ref, grad_ref, feed_ref, out_ref):
    core = where_ref[2]
    for m in range(2):
        high, low = split(jnp.where(core == m, mine_ref[...], other_ref[...]) * (1.0 / 32))
        first = jnp.concatenate([high, low], axis=1)
        second = jnp.concatenate([high, jnp.zeros_like(low)], axis=1)
        stack = jnp.concatenate([first, second], axis=0)
        for j in range(grad_ref.shape[2] // CHUNK):
            s_high, s_low = split(grad_ref[m, :, cols(j)].astype(f32) + feed_ref[m, :, cols(j)])
            wide = dot(jnp.concatenate([s_high, s_low], axis=0), stack, ((0,), (0,)))
            out_ref[m ^ core, cols(j), :] = wide[:, :RANK] + wide[:, RANK:]


def finish_kernel(part_ref, inverse_ref, out_ref):
    total = part_ref[0]
    for i in range(1, part_ref.shape[0]):
        total = total + part_ref[i]
    done = exact_dot(total * (1.0 / 32), inverse_ref[...], ((1,), (1,)))
    for i in range(part_ref.shape[0]):
        out_ref[i] = done


def update_kernel(slot, where_ref, basis_ref, right_ref, grad_ref, feed_ref, *rest):
    out_hbm, right_hbm, out_ref, sems = rest[2 * slot :]
    m = where_ref[2] ^ slot
    copies = [pltpu.make_async_copy(right_ref, right_hbm.at[m], sems.at[0])]
    copies[0].start()
    high, low = split(basis_ref[...])
    wide = jnp.concatenate([high, low], axis=1)
    for j in range(right_ref.shape[0] // CHUNK):
        r_high, r_low = split(right_ref[cols(j), :])
        rebuilt = dot(wide, jnp.concatenate([r_high, r_high], axis=1), ((1,), (1,)))
        rebuilt = rebuilt + dot(high, r_low, ((1,), (1,)))
        out_ref[:, cols(j)] = grad_ref[m, :, cols(j)].astype(f32) + feed_ref[m, :, cols(j)] - rebuilt
        copy = pltpu.make_async_copy(out_ref.at[:, cols(j)], out_hbm.at[m, :, cols(j)], sems.at[1 + j])
        copy.start()
        copies.append(copy)
    for copy in copies:
        copy.wait()


def update(slot, where, basis, right, gradients, feedback, previous=()):
    mats, rows, columns = gradients.shape
    return pl.pallas_call(
        functools.partial(update_kernel, slot),
        in_specs=[smem, vmem, vmem, vmem, vmem] + [hbm] * len(previous),
        out_specs=[hbm, hbm],
        out_shape=[
            jax.ShapeDtypeStruct((mats, rows, columns), f32),
            jax.ShapeDtypeStruct((mats, columns, RANK), f32),
        ],
        scratch_shapes=[
            pltpu.VMEM((rows, columns), f32),
            pltpu.SemaphoreType.DMA((1 + columns // CHUNK,)),
        ],
        input_output_aliases={5: 0, 6: 1} if previous else {},
        cost_estimate=pl.CostEstimate(flops=6 * rows * columns * RANK, bytes_accessed=8 * rows * columns, transcendentals=0),
        compiler_params=pltpu.CompilerParams(vmem_limit_bytes=8 * MIB),
        name=("update_mine", "update_other")[slot],
    )(where, basis, right, gradients, feedback, *previous)


def spread(x, axes, count):
    return lax.all_to_all(jnp.broadcast_to(x[None], (count,) + x.shape), axes, 0, 0)


def swap(x):
    return lax.ppermute(x, "core", [(0, 1), (1, 0)])


def on_device(gradients, feedback, seed_value):
    gradients, feedback = gradients[0], feedback[0]
    mats, rows, columns = gradients.shape
    chips = SIDE * SIDE
    depth = lax.axis_size("z")
    core = lax.axis_index("core")
    where = jnp.stack([seed_value[0], lax.axis_index("z") * columns, core]).astype(jnp.int32)

    left_part = pl.pallas_call(
        left_kernel,
        in_specs=[smem, hbm, hbm],
        out_specs=vmem,
        out_shape=jax.ShapeDtypeStruct((mats, rows, RANK), f32),
        scratch_shapes=[
            pltpu.VMEM((mats, rows, columns), bf16),
            pltpu.VMEM((mats, rows, columns), f32),
            pltpu.VMEM((columns, 2 * RANK), bf16),
            pltpu.SemaphoreType.DMA((columns // CHUNK, 2)),
        ],
        compiler_params=pltpu.CompilerParams(vmem_limit_bytes=62 * MIB),
        name="left_part",
    )(where, gradients, feedback)

    left = left_part[0] + swap(left_part[1])
    left = lax.all_to_all(left.reshape(chips, rows // chips, RANK), ("x", "y"), 0, 0).sum(0)
    left = spread(left, "z", depth).sum(0)
    left_mine = spread(left, ("x", "y"), chips).reshape(rows, RANK)
    left_other = swap(left_mine)

    right_part = pl.pallas_call(
        right_kernel,
        in_specs=[smem, vmem, vmem, vmem, vmem],
        out_specs=vmem,
        out_shape=jax.ShapeDtypeStruct((mats, columns, RANK), f32),
        cost_estimate=pl.CostEstimate(
            flops=12 * rows * columns * RANK, bytes_accessed=12 * rows * columns, transcendentals=0
        ),
        compiler_params=pltpu.CompilerParams(vmem_limit_bytes=8 * MIB),
        name="right_part",
    )(where, left_mine, left_other, gradients, feedback)

    basis_mine, inverse = pl.pallas_call(
        basis_kernel,
        in_specs=[vmem],
        out_specs=[vmem, vmem],
        out_shape=[jax.ShapeDtypeStruct((rows, RANK), f32), jax.ShapeDtypeStruct((RANK, RANK), f32)],
        cost_estimate=pl.CostEstimate(flops=6_000_000_000, bytes_accessed=400_000, transcendentals=0),
        compiler_params=pltpu.CompilerParams(vmem_limit_bytes=8 * MIB),
        name="basis",
    )(left_mine)
    basis_other = swap(basis_mine)
    mine_first = jnp.where(core == 0, basis_mine, basis_other)
    mine_last = jnp.where(core == 0, basis_other, basis_mine)
    left_basis = jnp.stack([mine_first, mine_last])

    right = right_part[0] + swap(right_part[1])
    right = lax.all_to_all(right.reshape(chips, columns // chips, RANK), ("x", "y"), 0, 0)
    right = pl.pallas_call(
        finish_kernel,
        in_specs=[vmem, vmem],
        out_specs=vmem,
        out_shape=jax.ShapeDtypeStruct(right.shape, f32),
        compiler_params=pltpu.CompilerParams(vmem_limit_bytes=8 * MIB),
        name="finish",
    )(right, inverse)
    right_mine = lax.all_to_all(right, ("x", "y"), 0, 0).reshape(columns, RANK)
    right_other = swap(right_mine)

    outs = update(0, where, basis_mine, right_mine, gradients, feedback)
    new_feedback, right_factor = update(1, where, basis_other, right_other, gradients, feedback, outs)
    return new_feedback[None], left_basis, right_factor


def solution(mesh):
    fine = Mesh(mesh.devices.reshape(SIDE, SIDE, CORES, -1), ("x", "y", "core", "z"))
    dp = ("x", "y", "core")
    placed = (P(dp, None, None, "z"), P(dp, None, None, "z"), P())
    return jax.shard_map(
        on_device,
        mesh=fine,
        in_specs=placed,
        out_specs=(P(dp, None, None, "z"), P(), P(None, "z", None)),
        check_vma=False,
    )
```

```python
import functools

import jax
import jax.numpy as jnp
from jax import lax
from jax.experimental import pallas as pl
from jax.experimental.pallas import tpu as pltpu
from jax.sharding import Mesh, PartitionSpec as P

RANK = 128
PRIME = 32749
SIDE = 4
CORES = 2
CHUNK = 256
GROUP = 8
MIB = 1024 * 1024

unit_scale = 3.4641016
f32 = jnp.float32
bf16 = jnp.bfloat16

smem = pl.BlockSpec(memory_space=pltpu.SMEM)
hbm = pl.BlockSpec(memory_space=pltpu.HBM)
vmem = pl.BlockSpec(memory_space=pltpu.VMEM)


def split(x):
    high = x.astype(bf16)
    return high, (x - high.astype(f32)).astype(bf16)


def dot(a, b, contract=((1,), (0,))):
    return lax.dot_general(a, b, (contract, ((), ())), preferred_element_type=f32)


def exact_dot(a, b, contract):
    return lax.dot_general(
        a, b, (contract, ((), ())), precision=lax.Precision.HIGHEST, preferred_element_type=f32
    )


def cols(j):
    return pl.ds(j * CHUNK, CHUNK)


def centred(x):
    quotient = (x.astype(f32) * (1.0 / PRIME) + 0.5).astype(jnp.int32)
    return x - quotient * PRIME


def start_block(seed, first, columns):
    col = first + lax.broadcasted_iota(jnp.int32, (columns, RANK), 0)
    rank = lax.broadcasted_iota(jnp.int32, (columns, RANK), 1)
    hashed = centred(col * 131 + rank * 977 + seed)
    hashed = centred(hashed * hashed + rank * 17 + 7)
    hashed = centred(hashed * hashed + col)
    hashed = jnp.where(hashed < 0, hashed + PRIME, hashed)
    return (hashed.astype(f32) * (1.0 / PRIME) - 0.5) * unit_scale


def left_kernel(seed_ref, grad_hbm, feed_hbm, mine_ref, other_ref, sum_ref, grad_ref, start_ref, sems):
    steps = grad_ref.shape[2] // CHUNK
    seed = seed_ref[0]
    first = lax.axis_index("z") * grad_ref.shape[2]
    core = lax.axis_index("core")
    copies = []
    for j in range(steps):
        pair = (
            pltpu.make_async_copy(grad_hbm.at[:, :, cols(j)], grad_ref.at[:, :, cols(j)], sems.at[j, 0]),
            pltpu.make_async_copy(feed_hbm.at[:, :, cols(j)], sum_ref.at[:, :, cols(j)], sems.at[j, 1]),
        )
        for copy in pair:
            copy.start()
        copies.append(pair)
    for j in range(steps):
        high, low = split(start_block(seed, first + j * CHUNK, CHUNK))
        start_ref[cols(j), :RANK] = high
        start_ref[cols(j), RANK:] = low
    for j in range(steps):
        for copy in copies[j]:
            copy.wait()
        both = start_ref[cols(j), :]
        for slot, ref in enumerate((mine_ref, other_ref)):
            m = core ^ slot
            summed = grad_ref[m, :, cols(j)].astype(f32) + sum_ref[m, :, cols(j)]
            sum_ref[m, :, cols(j)] = summed
            s_high, s_low = split(summed)
            wide = dot(s_high, both)
            part = wide[:, :RANK] + wide[:, RANK:] + dot(s_low, both[:, :RANK])
            if j == 0:
                ref[...] = part
            else:
                ref[...] += part


def eliminate(gram):
    lane = lax.broadcasted_iota(jnp.int32, (1, RANK), 1)
    count = RANK // GROUP
    blocks = [gram[GROUP * b : GROUP * (b + 1), :] for b in range(count)]
    sub = lax.broadcasted_iota(jnp.int32, (GROUP, RANK), 0)
    pivots = []
    for b in range(count):
        start = GROUP * b
        panel = blocks[b]
        spread_cols = [jnp.broadcast_to(panel[:, start + t : start + t + 1], (GROUP, RANK)) for t in range(GROUP)]
        a = [[spread_cols[t][s : s + 1, :] for t in range(GROUP)] for s in range(GROUP)]
        factors = [[None] * GROUP for _ in range(GROUP)]
        inverses = []
        for t in range(GROUP):
            pivots.append(a[t][t])
            inverses.append(1.0 / a[t][t])
            for s in range(t + 1, GROUP):
                factors[s][t] = a[s][t] * inverses[t]
                for u in range(t + 1, GROUP):
                    a[s][u] = a[s][u] - factors[s][t] * a[t][u]
        rows, sources = [], []
        for s in range(GROUP):
            row = panel[s : s + 1, :]
            for t in range(s):
                row = jnp.where(lane == start + t, 0.0, row) - factors[s][t] * sources[t]
            rows.append(row)
            sources.append(jnp.where(lane == start + s, 1.0, row))
        for s in range(GROUP):
            panel = jnp.where(sub == s, rows[s], panel)
        blocks[b] = panel
        for later in range(b + 1, count):
            block = blocks[later]
            heads = [jnp.broadcast_to(block[:, start + t : start + t + 1], (GROUP, RANK)) for t in range(GROUP)]
            for t in range(GROUP):
                factor = heads[t] * inverses[t]
                for u in range(t + 1, GROUP):
                    heads[u] = heads[u] - factor * a[t][u]
                block = jnp.where(lane == start + t, 0.0, block) - factor * sources[t]
            blocks[later] = block
    return jnp.concatenate(blocks, axis=0), jnp.concatenate(pivots, axis=0)


def basis_kernel(mine_ref, other_ref, right_ref, basis_ref, inverse_ref):
    del right_ref
    core = lax.axis_index("core")
    i = lax.broadcasted_iota(jnp.int32, (RANK, RANK), 0)
    j = lax.broadcasted_iota(jnp.int32, (RANK, RANK), 1)
    for slot, ref in enumerate((mine_ref, other_ref)):
        left = ref[...] * (1.0 / 32)
        lower, pivots = eliminate(exact_dot(left, left, ((0,), (0,))))
        inverse = jnp.where(i > j, lower, jnp.where(i == j, 1.0, 0.0)) * lax.rsqrt(pivots)
        if slot == 0:
            inverse_ref[...] = inverse
        basis_ref[core ^ slot] = exact_dot(left, inverse, ((1,), (1,)))


def right_kernel(slot, left_ref, sum_ref, out_ref):
    m = lax.axis_index("core") ^ slot
    high, low = split(left_ref[...] * (1.0 / 32))
    first = jnp.concatenate([high, low], axis=1)
    second = jnp.concatenate([high, jnp.zeros_like(low)], axis=1)
    stack = jnp.concatenate([first, second], axis=0)
    for j in range(sum_ref.shape[2] // CHUNK):
        s_high, s_low = split(sum_ref[m, :, cols(j)])
        wide = dot(jnp.concatenate([s_high, s_low], axis=0), stack, ((0,), (0,)))
        out_ref[cols(j), :] = wide[:, :RANK] + wide[:, RANK:]


def finish_kernel(part_ref, inverse_ref, out_ref):
    total = part_ref[0]
    for i in range(1, part_ref.shape[0]):
        total = total + part_ref[i]
    done = exact_dot(total * (1.0 / 32), inverse_ref[...], ((1,), (1,)))
    for i in range(part_ref.shape[0]):
        out_ref[i] = done


def update_kernel(slot, basis_ref, right_ref, sum_ref, *rest):
    out_hbm, right_hbm, out_ref, sems = rest[2 * slot :]
    m = lax.axis_index("core") ^ slot
    copies = [pltpu.make_async_copy(right_ref, right_hbm.at[m], sems.at[0])]
    copies[0].start()
    high, low = split(basis_ref[m])
    wide = jnp.concatenate([high, low], axis=1)
    for j in range(right_ref.shape[0] // CHUNK):
        r_high, r_low = split(right_ref[cols(j), :])
        rebuilt = dot(wide, jnp.concatenate([r_high, r_high], axis=1), ((1,), (1,)))
        rebuilt = rebuilt + dot(high, r_low, ((1,), (1,)))
        out_ref[:, cols(j)] = sum_ref[m, :, cols(j)] - rebuilt
        copy = pltpu.make_async_copy(out_ref.at[:, cols(j)], out_hbm.at[m, :, cols(j)], sems.at[1 + j])
        copy.start()
        copies.append(copy)
    for copy in copies:
        copy.wait()


def params(mib):
    return pltpu.CompilerParams(vmem_limit_bytes=mib * MIB)


def right_part(slot, left, summed):
    _, rows, columns = summed.shape
    return pl.pallas_call(
        functools.partial(right_kernel, slot),
        in_specs=[vmem, vmem],
        out_specs=vmem,
        out_shape=pltpu.VMEM((columns, RANK), f32),
        cost_estimate=pl.CostEstimate(
            flops=6 * rows * columns * RANK, bytes_accessed=4 * rows * columns, transcendentals=0
        ),
        compiler_params=params(8),
        name=("right_mine", "right_other")[slot],
    )(left, summed)


def update(slot, basis, right, summed, previous=()):
    mats, rows, columns = summed.shape
    return pl.pallas_call(
        functools.partial(update_kernel, slot),
        in_specs=[vmem, vmem, vmem] + [hbm] * len(previous),
        out_specs=[hbm, hbm],
        out_shape=[
            jax.ShapeDtypeStruct((mats, rows, columns), f32),
            jax.ShapeDtypeStruct((mats, columns, RANK), f32),
        ],
        scratch_shapes=[
            pltpu.VMEM((rows, columns), f32),
            pltpu.SemaphoreType.DMA((1 + columns // CHUNK,)),
        ],
        input_output_aliases={3: 0, 4: 1} if previous else {},
        cost_estimate=pl.CostEstimate(
            flops=6 * rows * columns * RANK, bytes_accessed=8 * rows * columns, transcendentals=0
        ),
        compiler_params=params(8),
        name=("update_mine", "update_other")[slot],
    )(basis, right, summed, *previous)


def spread(x, axes, count):
    return lax.all_to_all(jnp.broadcast_to(x[None], (count,) + x.shape), axes, 0, 0)


def swap(x):
    return lax.ppermute(x, "core", [(0, 1), (1, 0)])


def on_device(gradients, feedback, seed_value):
    gradients, feedback = gradients[0], feedback[0]
    mats, rows, columns = gradients.shape
    chips = SIDE * SIDE
    depth = lax.axis_size("z")

    mine, other, summed = pl.pallas_call(
        left_kernel,
        in_specs=[smem, hbm, hbm],
        out_specs=[vmem, vmem, vmem],
        out_shape=[
            pltpu.VMEM((rows, RANK), f32),
            pltpu.VMEM((rows, RANK), f32),
            pltpu.VMEM((mats, rows, columns), f32),
        ],
        scratch_shapes=[
            pltpu.VMEM((mats, rows, columns), bf16),
            pltpu.VMEM((columns, 2 * RANK), bf16),
            pltpu.SemaphoreType.DMA((columns // CHUNK, 2)),
        ],
        compiler_params=params(12),
        name="left_part",
    )(
        seed_value,
        pltpu.with_memory_space_constraint(gradients, pltpu.HBM),
        pltpu.with_memory_space_constraint(feedback, pltpu.HBM),
    )

    left = mine + swap(other)
    left = lax.all_to_all(left.reshape(chips, rows // chips, RANK), ("x", "y"), 0, 0).sum(0)
    left = spread(left, "z", depth).sum(0)
    left_mine = spread(left, ("x", "y"), chips).reshape(rows, RANK)
    left_other = swap(left_mine)

    sent = swap(right_part(1, left_other, summed))
    right = right_part(0, left_mine, summed) + sent
    left_basis, inverse = pl.pallas_call(
        basis_kernel,
        in_specs=[vmem, vmem, pl.BlockSpec(memory_space=pl.ANY)],
        out_specs=[vmem, vmem],
        out_shape=[jax.ShapeDtypeStruct((mats, rows, RANK), f32), pltpu.VMEM((RANK, RANK), f32)],
        cost_estimate=pl.CostEstimate(flops=10_000_000_000, bytes_accessed=800_000, transcendentals=0),
        compiler_params=params(8),
        name="basis",
    )(left_mine, left_other, right)
    right = lax.all_to_all(right.reshape(chips, columns // chips, RANK), ("x", "y"), 0, 0)
    right = pl.pallas_call(
        finish_kernel,
        in_specs=[vmem, vmem],
        out_specs=vmem,
        out_shape=pltpu.VMEM(right.shape, f32),
        compiler_params=params(8),
        name="finish",
    )(right, inverse)
    right_mine = lax.all_to_all(right, ("x", "y"), 0, 0).reshape(columns, RANK)
    right_other = swap(right_mine)

    outs = update(0, left_basis, right_mine, summed)
    new_feedback, right_factor = update(1, left_basis, right_other, summed, outs)
    return new_feedback[None], left_basis, right_factor


def solution(mesh):
    fine = Mesh(mesh.devices.reshape(SIDE, SIDE, CORES, -1), ("x", "y", "core", "z"))
    dp = ("x", "y", "core")
    placed = (P(dp, None, None, "z"), P(dp, None, None, "z"), P())
    return jax.shard_map(
        on_device,
        mesh=fine,
        in_specs=placed,
        out_specs=(P(dp, None, None, "z"), P(), P(None, "z", None)),
        check_vma=False,
    )
```

```python
import functools

import jax
import jax.numpy as jnp
from jax import lax
from jax.experimental import pallas as pl
from jax.experimental.pallas import tpu as pltpu
from jax.sharding import Mesh, PartitionSpec as P

RANK = 128
PRIME = 32749
SIDE = 4
CORES = 2
CHUNK = 256
GROUP = 8
TILE = 8
MIB = 1024 * 1024

unit_scale = 3.4641016
f32 = jnp.float32
bf16 = jnp.bfloat16

smem = pl.BlockSpec(memory_space=pltpu.SMEM)
hbm = pl.BlockSpec(memory_space=pltpu.HBM)
vmem = pl.BlockSpec(memory_space=pltpu.VMEM)


def split(x):
    high = x.astype(bf16)
    return high, (x - high.astype(f32)).astype(bf16)


def dot(a, b, contract=((1,), (0,))):
    return lax.dot_general(a, b, (contract, ((), ())), preferred_element_type=f32)


def exact_dot(a, b, contract):
    return lax.dot_general(
        a, b, (contract, ((), ())), precision=lax.Precision.HIGHEST, preferred_element_type=f32
    )


def cols(j):
    return pl.ds(j * CHUNK, CHUNK)


def centred(x):
    quotient = (x.astype(f32) * (1.0 / PRIME) + 0.5).astype(jnp.int32)
    return x - quotient * PRIME


def start_block(seed, first, columns):
    col = first + lax.broadcasted_iota(jnp.int32, (columns, RANK), 0)
    rank = lax.broadcasted_iota(jnp.int32, (columns, RANK), 1)
    hashed = centred(col * 131 + rank * 977 + seed)
    hashed = centred(hashed * hashed + rank * 17 + 7)
    hashed = centred(hashed * hashed + col)
    hashed = jnp.where(hashed < 0, hashed + PRIME, hashed)
    return (hashed.astype(f32) * (1.0 / PRIME) - 0.5) * unit_scale


def left_kernel(seed_ref, grad_hbm, feed_hbm, mine_ref, other_ref, mine_sum_ref, other_sum_ref, grad_ref, start_ref, sems):
    _, rows, columns = grad_ref.shape
    steps = columns // CHUNK
    slots = ((mine_ref, mine_sum_ref), (other_ref, other_sum_ref))
    first = lax.axis_index("z") * columns
    core = lax.axis_index("core")
    copies = []
    for j in range(steps):
        group = [pltpu.make_async_copy(grad_hbm.at[:, :, cols(j)], grad_ref.at[:, :, cols(j)], sems.at[j, 0])]
        for slot, (_, sum_ref) in enumerate(slots):
            source = feed_hbm.at[core ^ slot, :, cols(j)]
            group.append(pltpu.make_async_copy(source, sum_ref.at[:, cols(j)], sems.at[j, 1 + slot]))
        for copy in group:
            copy.start()
        copies.append(group)
    for ref, _ in slots:
        ref[rows:, :] = jnp.zeros((ref.shape[0] - rows, RANK), f32)
    seed = seed_ref[0]
    for j in range(steps):
        high, low = split(start_block(seed, first + j * CHUNK, CHUNK))
        start_ref[cols(j), :RANK] = high
        start_ref[cols(j), RANK:] = low
    for j in range(steps):
        for copy in copies[j]:
            copy.wait()
        both = start_ref[cols(j), :]
        for slot, (ref, sum_ref) in enumerate(slots):
            summed = grad_ref[core ^ slot, :, cols(j)].astype(f32) + sum_ref[:, cols(j)]
            sum_ref[:, cols(j)] = summed
            s_high, s_low = split(summed)
            wide = dot(s_high, both)
            part = wide[:, :RANK] + wide[:, RANK:] + dot(s_low, both[:, :RANK])
            if j == 0:
                ref[:rows, :] = part
            else:
                ref[:rows, :] += part


def eliminate(gram):
    lane = lax.broadcasted_iota(jnp.int32, (1, RANK), 1)
    count = RANK // GROUP
    blocks = [gram[GROUP * b : GROUP * (b + 1), :] for b in range(count)]
    sub = lax.broadcasted_iota(jnp.int32, (GROUP, RANK), 0)
    pivots = []
    for b in range(count):
        start = GROUP * b
        panel = blocks[b]
        spread_cols = [jnp.broadcast_to(panel[:, start + t : start + t + 1], (GROUP, RANK)) for t in range(GROUP)]
        a = [[spread_cols[t][s : s + 1, :] for t in range(GROUP)] for s in range(GROUP)]
        factors = [[None] * GROUP for _ in range(GROUP)]
        inverses = []
        for t in range(GROUP):
            pivots.append(a[t][t])
            inverses.append(1.0 / a[t][t])
            for s in range(t + 1, GROUP):
                factors[s][t] = a[s][t] * inverses[t]
                for u in range(t + 1, GROUP):
                    a[s][u] = a[s][u] - factors[s][t] * a[t][u]
        rows, sources = [], []
        for s in range(GROUP):
            row = panel[s : s + 1, :]
            for t in range(s):
                row = jnp.where(lane == start + t, 0.0, row) - factors[s][t] * sources[t]
            rows.append(row)
            sources.append(jnp.where(lane == start + s, 1.0, row))
        for s in range(GROUP):
            panel = jnp.where(sub == s, rows[s], panel)
        blocks[b] = panel
        for later in range(b + 1, count):
            block = blocks[later]
            heads = [jnp.broadcast_to(block[:, start + t : start + t + 1], (GROUP, RANK)) for t in range(GROUP)]
            for t in range(GROUP):
                factor = heads[t] * inverses[t]
                for u in range(t + 1, GROUP):
                    heads[u] = heads[u] - factor * a[t][u]
                block = jnp.where(lane == start + t, 0.0, block) - factor * sources[t]
            blocks[later] = block
    return jnp.concatenate(blocks, axis=0), jnp.concatenate(pivots, axis=0)


def basis_kernel(mine_ref, other_ref, right_ref, basis_ref, inverse_ref):
    del right_ref
    core = lax.axis_index("core")
    i = lax.broadcasted_iota(jnp.int32, (RANK, RANK), 0)
    j = lax.broadcasted_iota(jnp.int32, (RANK, RANK), 1)
    for slot, ref in enumerate((mine_ref, other_ref)):
        left = ref[: basis_ref.shape[1], :] * (1.0 / 32)
        lower, pivots = eliminate(exact_dot(left, left, ((0,), (0,))))
        inverse = jnp.where(i > j, lower, jnp.where(i == j, 1.0, 0.0)) * lax.rsqrt(pivots)
        if slot == 0:
            inverse_ref[...] = inverse
        basis_ref[core ^ slot] = exact_dot(left, inverse, ((1,), (1,)))


def right_kernel(left_ref, *rest):
    keeps = []
    if len(rest) == 2:
        sum_ref, out_ref = rest
    else:
        sum_ref, other_ref, out_ref, sum_hbm, other_hbm, sems = rest
        keeps = [
            pltpu.make_async_copy(sum_ref, sum_hbm, sems.at[0]),
            pltpu.make_async_copy(other_ref, other_hbm, sems.at[1]),
        ]
    for keep in keeps:
        keep.start()
    rows, columns = sum_ref.shape
    high, low = split(left_ref[:rows, :] * (1.0 / 32))
    first = jnp.concatenate([high, low], axis=1)
    second = jnp.concatenate([high, jnp.zeros_like(low)], axis=1)
    stack = jnp.concatenate([first, second], axis=0)
    for j in range(columns // CHUNK):
        s_high, s_low = split(sum_ref[:, cols(j)])
        wide = dot(jnp.concatenate([s_high, s_low], axis=0), stack, ((0,), (0,)))
        out_ref[cols(j), :] = wide[:, :RANK] + wide[:, RANK:]
    for keep in keeps:
        keep.wait()


def finish_kernel(part_ref, inverse_ref, out_ref):
    total = part_ref[0]
    for i in range(1, part_ref.shape[0]):
        total = total + part_ref[i]
    done = exact_dot(total * (1.0 / 32), inverse_ref[...], ((1,), (1,)))
    for i in range(part_ref.shape[0]):
        out_ref[i] = done


def update_kernel(slot, basis_ref, right_ref, sum_ref, *rest):
    out_hbm, right_hbm, out_ref, sems = rest[2 * slot :]
    m = lax.axis_index("core") ^ slot
    copies = [pltpu.make_async_copy(right_ref, right_hbm.at[m], sems.at[0])]
    copies[0].start()
    high, low = split(basis_ref[m])
    wide = jnp.concatenate([high, low], axis=1)
    for j in range(right_ref.shape[0] // CHUNK):
        r_high, r_low = split(right_ref[cols(j), :])
        rebuilt = dot(wide, jnp.concatenate([r_high, r_high], axis=1), ((1,), (1,)))
        rebuilt = rebuilt + dot(high, r_low, ((1,), (1,)))
        out_ref[:, cols(j)] = sum_ref[:, cols(j)] - rebuilt
        copy = pltpu.make_async_copy(out_ref.at[:, cols(j)], out_hbm.at[m, :, cols(j)], sems.at[1 + j])
        copy.start()
        copies.append(copy)
    for copy in copies:
        copy.wait()


def params(mib):
    return pltpu.CompilerParams(vmem_limit_bytes=mib * MIB)


def right_part(name, left, *summed):
    rows, columns = summed[0].shape
    kept = len(summed) if len(summed) > 1 else 0
    out = pl.pallas_call(
        right_kernel,
        in_specs=[vmem] * (1 + len(summed)),
        out_specs=[vmem] + [hbm] * kept,
        out_shape=[pltpu.VMEM((columns, RANK), f32)] + [pltpu.HBM((rows, columns), f32)] * kept,
        scratch_shapes=[pltpu.SemaphoreType.DMA((kept,))] if kept else [],
        cost_estimate=pl.CostEstimate(
            flops=6 * rows * columns * RANK, bytes_accessed=4 * rows * columns, transcendentals=0
        ),
        compiler_params=params(8),
        name=name,
    )(left, *summed)
    return out if kept else out[0]


def update(slot, basis, right, summed, previous=()):
    mats = basis.shape[0]
    rows, columns = summed.shape
    return pl.pallas_call(
        functools.partial(update_kernel, slot),
        in_specs=[vmem, vmem, vmem] + [hbm] * len(previous),
        out_specs=[hbm, hbm],
        out_shape=[
            jax.ShapeDtypeStruct((mats, rows, columns), f32),
            jax.ShapeDtypeStruct((mats, columns, RANK), f32),
        ],
        scratch_shapes=[
            pltpu.VMEM((rows, columns), f32),
            pltpu.SemaphoreType.DMA((1 + columns // CHUNK,)),
        ],
        input_output_aliases={3: 0, 4: 1} if previous else {},
        cost_estimate=pl.CostEstimate(
            flops=6 * rows * columns * RANK, bytes_accessed=8 * rows * columns, transcendentals=0
        ),
        compiler_params=params(8),
        name=("update_mine", "update_other")[slot],
    )(basis, right, summed, *previous)


def sum_kernel(part_ref, out_ref):
    total = part_ref[0]
    for i in range(1, part_ref.shape[0]):
        total = total + part_ref[i]
    for i in range(out_ref.shape[0]):
        out_ref[i] = total


def sum_spread(parts, count):
    return pl.pallas_call(
        sum_kernel,
        in_specs=[vmem],
        out_specs=vmem,
        out_shape=pltpu.VMEM((count,) + parts.shape[1:], f32),
        compiler_params=params(4),
        name="sum_spread",
    )(parts)


def swap(x):
    return lax.ppermute(x, "core", [(0, 1), (1, 0)])


def on_device(gradients, feedback, seed_value):
    gradients, feedback = gradients[0], feedback[0]
    mats, rows, columns = gradients.shape
    chips = SIDE * SIDE
    depth = lax.axis_size("z")

    share = -(-rows // (chips * TILE)) * TILE
    padded = chips * share

    mine, other, mine_sum, other_sum = pl.pallas_call(
        left_kernel,
        in_specs=[smem, hbm, hbm],
        out_specs=[vmem] * 4,
        out_shape=[
            pltpu.VMEM((padded, RANK), f32),
            pltpu.VMEM((padded, RANK), f32),
            pltpu.VMEM((rows, columns), f32),
            pltpu.VMEM((rows, columns), f32),
        ],
        scratch_shapes=[
            pltpu.VMEM((mats, rows, columns), bf16),
            pltpu.VMEM((columns, 2 * RANK), bf16),
            pltpu.SemaphoreType.DMA((columns // CHUNK, 3)),
        ],
        compiler_params=params(12),
        name="left_part",
    )(
        seed_value,
        pltpu.with_memory_space_constraint(gradients, pltpu.HBM),
        pltpu.with_memory_space_constraint(feedback, pltpu.HBM),
    )

    left = mine + swap(other)
    left = lax.all_to_all(left.reshape(chips, share, RANK), ("x", "y"), 0, 0)
    left = lax.all_to_all(sum_spread(left, depth), "z", 0, 0)
    left_mine = lax.all_to_all(sum_spread(left, chips), ("x", "y"), 0, 0).reshape(padded, RANK)
    left_other = swap(left_mine)

    sent = swap(right_part("right_other", left_other, other_sum))
    right, mine_sum, other_sum = right_part("right_mine", left_mine, mine_sum, other_sum)
    right = right + sent
    left_basis, inverse = pl.pallas_call(
        basis_kernel,
        in_specs=[vmem, vmem, hbm],
        out_specs=[vmem, vmem],
        out_shape=[jax.ShapeDtypeStruct((mats, rows, RANK), f32), pltpu.VMEM((RANK, RANK), f32)],
        cost_estimate=pl.CostEstimate(flops=10_000_000_000, bytes_accessed=800_000, transcendentals=0),
        compiler_params=params(8),
        name="basis",
    )(left_mine, left_other, right)
    right = lax.all_to_all(right.reshape(chips, columns // chips, RANK), ("x", "y"), 0, 0)
    right = pl.pallas_call(
        finish_kernel,
        in_specs=[vmem, vmem],
        out_specs=vmem,
        out_shape=pltpu.VMEM(right.shape, f32),
        compiler_params=params(8),
        name="finish",
    )(right, inverse)
    right_mine = lax.all_to_all(right, ("x", "y"), 0, 0).reshape(columns, RANK)
    right_other = swap(right_mine)

    outs = update(0, left_basis, right_mine, mine_sum)
    new_feedback, right_factor = update(1, left_basis, right_other, other_sum, outs)
    return new_feedback[None], left_basis, right_factor


def solution(mesh):
    fine = Mesh(mesh.devices.reshape(SIDE, SIDE, CORES, -1), ("x", "y", "core", "z"))
    dp = ("x", "y", "core")
    placed = (P(dp, None, None, "z"), P(dp, None, None, "z"), P())
    return jax.shard_map(
        on_device,
        mesh=fine,
        in_specs=placed,
        out_specs=(P(dp, None, None, "z"), P(), P(None, "z", None)),
        check_vma=False,
    )
```

```python
import functools

import jax
import jax.numpy as jnp
from jax import lax
from jax.experimental import pallas as pl
from jax.experimental.pallas import tpu as pltpu
from jax.sharding import Mesh, PartitionSpec as P

RANK = 128
PRIME = 32749
CHIPS = 16
CHUNK = 256
LANES = 128
GROUP = 8
TILE = 8
MIB = 1024 * 1024

unit_scale = 3.4641016
f32 = jnp.float32
bf16 = jnp.bfloat16

smem = pl.BlockSpec(memory_space=pltpu.SMEM)
hbm = pl.BlockSpec(memory_space=pltpu.HBM)
vmem = pl.BlockSpec(memory_space=pltpu.VMEM)

PLANE = ("xh", "xl", "yh", "yl")


def split(x):
    high = x.astype(bf16)
    return high, (x - high.astype(f32)).astype(bf16)


def dot(a, b, contract=((1,), (0,))):
    return lax.dot_general(a, b, (contract, ((), ())), preferred_element_type=f32)


def exact_dot(a, b, contract):
    return lax.dot_general(
        a, b, (contract, ((), ())), precision=lax.Precision.HIGHEST, preferred_element_type=f32
    )


def cols(j):
    return pl.ds(j * CHUNK, CHUNK)


def params(mib):
    return pltpu.CompilerParams(vmem_limit_bytes=mib * MIB)


def centred(x):
    quotient = (x.astype(f32) * (1.0 / PRIME) + 0.5).astype(jnp.int32)
    return x - quotient * PRIME


def start_block(seed, first, columns):
    col = first + lax.broadcasted_iota(jnp.int32, (columns, RANK), 0)
    rank = lax.broadcasted_iota(jnp.int32, (columns, RANK), 1)
    hashed = centred(col * 131 + rank * 977 + seed)
    hashed = centred(hashed * hashed + rank * 17 + 7)
    hashed = centred(hashed * hashed + col)
    hashed = jnp.where(hashed < 0, hashed + PRIME, hashed)
    return (hashed.astype(f32) * (1.0 / PRIME) - 0.5) * unit_scale


def places(tile):
    xh, xl, yh, yl = tile >> 3, (tile >> 2) & 1, (tile >> 1) & 1, tile & 1
    rest = 2 * xh + yh
    far_x, far_y = xl ^ lax.axis_index("xl"), yl ^ lax.axis_index("yl")
    return 8 * far_x + 4 * far_y + rest, 8 * far_y + 4 * far_x + rest


def left_kernel(seed_ref, grad_hbm, feed_hbm, *refs):
    lefts, uppers, lowers, sums = (refs[n : n + 2] for n in range(0, 8, 2))
    grad_ref, feed_ref, start_ref, sems = refs[8:]
    _, rows, columns = grad_ref.shape
    half = rows // 2
    steps = columns // CHUNK
    seed = seed_ref[0]
    first = lax.axis_index("z") * columns
    core = lax.axis_index("core")
    copies = []
    for j in range(steps):
        pair = (
            pltpu.make_async_copy(grad_hbm.at[:, :, cols(j)], grad_ref.at[:, :, cols(j)], sems.at[j, 0]),
            pltpu.make_async_copy(feed_hbm.at[:, :, cols(j)], feed_ref.at[:, :, cols(j)], sems.at[j, 1]),
        )
        for copy in pair:
            copy.start()
        copies.append(pair)
    for left_ref in lefts:
        left_ref[rows:, :] = jnp.zeros((left_ref.shape[0] - rows, RANK), f32)
    for tile in range(columns // LANES, CHIPS):
        upper, lower = places(tile)
        for slot in range(2):
            uppers[slot][upper] = jnp.zeros((half, LANES), f32)
            lowers[slot][lower] = jnp.zeros((half, LANES), f32)
    for j in range(steps):
        high, low = split(start_block(seed, first + j * CHUNK, CHUNK))
        start_ref[cols(j), :RANK] = high
        start_ref[cols(j), RANK:] = low
    saves = []
    for j in range(steps):
        for copy in copies[j]:
            copy.wait()
        both = start_ref[cols(j), :]
        for slot in range(2):
            m = core ^ slot
            summed = grad_ref[m, :, cols(j)].astype(f32) + feed_ref[m, :, cols(j)]
            feed_ref[m, :, cols(j)] = summed
            save = pltpu.make_async_copy(feed_ref.at[m, :, cols(j)], sums[slot].at[:, cols(j)], sems.at[j, 2 + slot])
            save.start()
            saves.append(save)
            for part in range(CHUNK // LANES):
                upper, lower = places(j * (CHUNK // LANES) + part)
                span = slice(part * LANES, (part + 1) * LANES)
                uppers[slot][upper] = summed[:half, span]
                lowers[slot][lower] = summed[half:, span]
            s_high, s_low = split(summed)
            wide = dot(s_high, both)
            piece = wide[:, :RANK] + wide[:, RANK:] + dot(s_low, both[:, :RANK])
            if j == 0:
                lefts[slot][:rows, :] = piece
            else:
                lefts[slot][:rows, :] += piece
    for save in saves:
        save.wait()


def eliminate(gram):
    lane = lax.broadcasted_iota(jnp.int32, (1, RANK), 1)
    count = RANK // GROUP
    blocks = [gram[GROUP * b : GROUP * (b + 1), :] for b in range(count)]
    sub = lax.broadcasted_iota(jnp.int32, (GROUP, RANK), 0)
    pivots = []
    for b in range(count):
        start = GROUP * b
        panel = blocks[b]
        spread_cols = [jnp.broadcast_to(panel[:, start + t : start + t + 1], (GROUP, RANK)) for t in range(GROUP)]
        a = [[spread_cols[t][s : s + 1, :] for t in range(GROUP)] for s in range(GROUP)]
        factors = [[None] * GROUP for _ in range(GROUP)]
        inverses = []
        for t in range(GROUP):
            pivots.append(a[t][t])
            inverses.append(1.0 / a[t][t])
            for s in range(t + 1, GROUP):
                factors[s][t] = a[s][t] * inverses[t]
                for u in range(t + 1, GROUP):
                    a[s][u] = a[s][u] - factors[s][t] * a[t][u]
        rows, sources = [], []
        for s in range(GROUP):
            row = panel[s : s + 1, :]
            for t in range(s):
                row = jnp.where(lane == start + t, 0.0, row) - factors[s][t] * sources[t]
            rows.append(row)
            sources.append(jnp.where(lane == start + s, 1.0, row))
        for s in range(GROUP):
            panel = jnp.where(sub == s, rows[s], panel)
        blocks[b] = panel
        for later in range(b + 1, count):
            block = blocks[later]
            heads = [jnp.broadcast_to(block[:, start + t : start + t + 1], (GROUP, RANK)) for t in range(GROUP)]
            for t in range(GROUP):
                factor = heads[t] * inverses[t]
                for u in range(t + 1, GROUP):
                    heads[u] = heads[u] - factor * a[t][u]
                block = jnp.where(lane == start + t, 0.0, block) - factor * sources[t]
            blocks[later] = block
    return jnp.concatenate(blocks, axis=0), jnp.concatenate(pivots, axis=0)


def basis_kernel(left_ref, after_ref, basis_ref):
    del after_ref
    left = left_ref[: basis_ref.shape[0], :] * (1.0 / 32)
    lower, pivots = eliminate(exact_dot(left, left, ((0,), (0,))))
    i = lax.broadcasted_iota(jnp.int32, (RANK, RANK), 0)
    j = lax.broadcasted_iota(jnp.int32, (RANK, RANK), 1)
    inverse = jnp.where(i > j, lower, jnp.where(i == j, 1.0, 0.0)) * lax.rsqrt(pivots)
    basis_ref[...] = exact_dot(left, inverse, ((1,), (1,)))


def sum_kernel(part_ref, out_ref):
    total = part_ref[0]
    for i in range(1, part_ref.shape[0]):
        total = total + part_ref[i]
    for i in range(out_ref.shape[0]):
        out_ref[i] = total


def sum_spread(parts, count):
    return pl.pallas_call(
        sum_kernel,
        in_specs=[vmem],
        out_specs=vmem,
        out_shape=pltpu.VMEM((count,) + parts.shape[1:], f32),
        compiler_params=params(4),
        name="sum_spread",
    )(parts)


def halve_kernel(after_ref, *refs):
    del after_ref
    for side in range(2):
        kept_ref, got_ref = refs[2 * side : 2 * side + 2]
        keep_ref, send_ref = refs[4 + 2 * side : 6 + 2 * side]
        count = keep_ref.shape[0]
        for i in range(count):
            keep_ref[i] = kept_ref[i] + got_ref[i]
            send_ref[i] = kept_ref[count + i] + got_ref[count + i]


def halve(after, *blocks):
    shape = (blocks[0].shape[0] // 2,) + blocks[0].shape[1:]
    return pl.pallas_call(
        halve_kernel,
        in_specs=[hbm] + [vmem] * 4,
        out_specs=[vmem] * 4,
        out_shape=[pltpu.VMEM(shape, f32)] * 4,
        compiler_params=params(4),
        name="halve",
    )(after, *blocks)


def join_kernel(after_ref, upper_ref, upper_got_ref, lower_ref, lower_got_ref, out_ref):
    del after_ref
    half = upper_ref.shape[1]
    for i in range(out_ref.shape[0]):
        out_ref[i, :half, :] = upper_ref[i] + upper_got_ref[i]
        out_ref[i, half:, :] = lower_ref[i] + lower_got_ref[i]


def finish_kernel(part_ref, basis_ref, out_ref):
    total = part_ref[0]
    for i in range(1, part_ref.shape[0]):
        total = total + part_ref[i]
    right = exact_dot(total * (1.0 / 32), basis_ref[...], ((0,), (0,)))
    for i in range(out_ref.shape[0]):
        out_ref[i] = right


def update_kernel(slot, basis_ref, right_ref, sum_ref, *rest):
    out_hbm, right_hbm, basis_hbm, out_ref, sems = rest[3 * slot :]
    columns = sum_ref.shape[1]
    steps = columns // CHUNK
    m = lax.axis_index("core") ^ slot
    stores = [
        pltpu.make_async_copy(right_ref.at[:columns], right_hbm.at[m], sems.at[steps]),
        pltpu.make_async_copy(basis_ref, basis_hbm.at[m], sems.at[steps + 1]),
    ]
    for copy in stores:
        copy.start()
    high, low = split(basis_ref[...])
    wide = jnp.concatenate([high, low], axis=1)
    for j in range(steps):
        r_high, r_low = split(right_ref[cols(j), :])
        rebuilt = dot(wide, jnp.concatenate([r_high, r_high], axis=1), ((1,), (1,)))
        rebuilt = rebuilt + dot(high, r_low, ((1,), (1,)))
        out_ref[:, cols(j)] = sum_ref[:, cols(j)] - rebuilt
        copy = pltpu.make_async_copy(out_ref.at[:, cols(j)], out_hbm.at[m, :, cols(j)], sems.at[j])
        copy.start()
        stores.append(copy)
    for copy in stores:
        copy.wait()


def update(slot, basis, right, summed, previous=()):
    rows, columns = summed.shape
    return pl.pallas_call(
        functools.partial(update_kernel, slot),
        in_specs=[vmem] * 3 + [hbm] * len(previous),
        out_specs=[hbm] * 3,
        out_shape=[
            jax.ShapeDtypeStruct((2, rows, columns), f32),
            jax.ShapeDtypeStruct((2, columns, RANK), f32),
            jax.ShapeDtypeStruct((2, rows, RANK), f32),
        ],
        scratch_shapes=[
            pltpu.VMEM((rows, columns), f32),
            pltpu.SemaphoreType.DMA((2 + columns // CHUNK,)),
        ],
        input_output_aliases={3: 0, 4: 1, 5: 2} if previous else {},
        cost_estimate=pl.CostEstimate(
            flops=6 * rows * columns * RANK, bytes_accessed=8 * rows * columns, transcendentals=0
        ),
        compiler_params=params(8),
        name=("update_mine", "update_other")[slot],
    )(basis, right, summed, *previous)


def swap(x, axis="core"):
    return lax.ppermute(x, axis, [(0, 1), (1, 0)])


def exchange(x, axes=PLANE):
    return lax.all_to_all(x, axes, 0, 0)


def on_device(gradients, feedback, seed_value):
    gradients = pltpu.with_memory_space_constraint(gradients[0], pltpu.HBM)
    feedback = pltpu.with_memory_space_constraint(feedback[0], pltpu.HBM)
    mats, rows, columns = gradients.shape
    depth = lax.axis_size("z")
    share = -(-rows // (CHIPS * TILE)) * TILE
    padded = CHIPS * share

    mine, other, upper, upper_other, lower, lower_other, summed, summed_other = pl.pallas_call(
        left_kernel,
        in_specs=[smem, hbm, hbm],
        out_specs=[vmem] * 6 + [hbm] * 2,
        out_shape=[pltpu.VMEM((padded, RANK), f32)] * 2
        + [pltpu.VMEM((CHIPS, rows // 2, LANES), f32)] * 4
        + [pltpu.HBM((rows, columns), f32)] * 2,
        scratch_shapes=[
            pltpu.VMEM((mats, rows, columns), bf16),
            pltpu.VMEM((mats, rows, columns), f32),
            pltpu.VMEM((columns, 2 * RANK), bf16),
            pltpu.SemaphoreType.DMA((columns // CHUNK, 4)),
        ],
        compiler_params=params(20),
        name="left_part",
    )(seed_value, gradients, feedback)

    left = mine + swap(other)
    left, upper_other, lower_other = lax.optimization_barrier((left, upper_other, lower_other))
    upper_got, lower_got = swap(upper_other), swap(lower_other)
    left = exchange(left.reshape(CHIPS, share, RANK))
    upper, upper_send, lower, lower_send = halve(left, upper, upper_got, lower, lower_got)
    upper_got, lower_got = swap(upper_send, "xl"), swap(lower_send, "yl")
    left = exchange(sum_spread(left, depth), "z")
    upper, upper_send, lower, lower_send = halve(left, upper, upper_got, lower, lower_got)
    upper_got, lower_got = swap(upper_send, "yl"), swap(lower_send, "xl")
    left = exchange(sum_spread(left, CHIPS))

    quarter = pl.pallas_call(
        join_kernel,
        in_specs=[hbm] + [vmem] * 4,
        out_specs=vmem,
        out_shape=pltpu.VMEM((CHIPS // 4, rows, LANES), f32),
        compiler_params=params(4),
        name="join",
    )(left, upper, upper_got, lower, lower_got)
    basis = pl.pallas_call(
        basis_kernel,
        in_specs=[vmem, hbm],
        out_specs=vmem,
        out_shape=pltpu.VMEM((rows, RANK), f32),
        cost_estimate=pl.CostEstimate(flops=5_000_000_000, bytes_accessed=400_000, transcendentals=0),
        compiler_params=params(8),
        name="basis",
    )(left.reshape(padded, RANK), quarter)
    basis_other = swap(basis)
    right = pl.pallas_call(
        finish_kernel,
        in_specs=[vmem, vmem],
        out_specs=vmem,
        out_shape=pltpu.VMEM((CHIPS, LANES, RANK), f32),
        compiler_params=params(4),
        name="finish",
    )(exchange(quarter, ("xh", "yh")), basis)
    right = exchange(right).reshape(CHIPS * LANES, RANK)
    right_other = swap(right)

    outs = update(0, basis, right, summed)
    new_feedback, right_factor, left_basis = update(1, basis_other, right_other, summed_other, outs)
    return new_feedback[None], left_basis, right_factor


def solution(mesh):
    fine = Mesh(mesh.devices.reshape(2, 2, 2, 2, 2, -1), PLANE + ("core", "z"))
    dp = PLANE + ("core",)
    placed = (P(dp, None, None, "z"), P(dp, None, None, "z"), P())
    return jax.shard_map(
        on_device,
        mesh=fine,
        in_specs=placed,
        out_specs=(P(dp, None, None, "z"), P(), P(None, "z", None)),
        check_vma=False,
    )
```

```python
import functools

import jax
import jax.numpy as jnp
from jax import lax
from jax.experimental import pallas as pl
from jax.experimental.pallas import tpu as pltpu
from jax.sharding import Mesh, PartitionSpec as P

RANK = 128
PRIME = 32749
CHIPS = 16
CHUNK = 256
LANES = 128
GROUP = 8
TILE = 8
MIB = 1024 * 1024

unit_scale = 3.4641016
f32 = jnp.float32
bf16 = jnp.bfloat16

smem = pl.BlockSpec(memory_space=pltpu.SMEM)
hbm = pl.BlockSpec(memory_space=pltpu.HBM)
vmem = pl.BlockSpec(memory_space=pltpu.VMEM)

PLANE = ("xh", "xl", "yh", "yl")


def split(x):
    high = x.astype(bf16)
    return high, (x - high.astype(f32)).astype(bf16)


def dot(a, b, contract=((1,), (0,))):
    return lax.dot_general(a, b, (contract, ((), ())), preferred_element_type=f32)


def exact_dot(a, b, contract):
    return lax.dot_general(
        a, b, (contract, ((), ())), precision=lax.Precision.HIGHEST, preferred_element_type=f32
    )


def cols(j):
    return pl.ds(j * CHUNK, CHUNK)


def params(mib):
    return pltpu.CompilerParams(vmem_limit_bytes=mib * MIB)


def centred(x):
    quotient = (x.astype(f32) * (1.0 / PRIME) + 0.5).astype(jnp.int32)
    return x - quotient * PRIME


def start_block(seed, first, columns):
    col = first + lax.broadcasted_iota(jnp.int32, (columns, RANK), 0)
    rank = lax.broadcasted_iota(jnp.int32, (columns, RANK), 1)
    hashed = centred(col * 131 + rank * 977 + seed)
    hashed = centred(hashed * hashed + rank * 17 + 7)
    hashed = centred(hashed * hashed + col)
    hashed = jnp.where(hashed < 0, hashed + PRIME, hashed)
    return (hashed.astype(f32) * (1.0 / PRIME) - 0.5) * unit_scale


def places(tile):
    xh, xl, yh, yl = tile >> 3, (tile >> 2) & 1, (tile >> 1) & 1, tile & 1
    rest = 2 * xl + yl
    far_x, far_y = xh ^ lax.axis_index("xh"), yh ^ lax.axis_index("yh")
    return 8 * far_x + 4 * far_y + rest, 8 * far_y + 4 * far_x + rest


def left_kernel(seed_ref, grad_hbm, feed_hbm, *refs):
    lefts, uppers, lowers, sums = (refs[n : n + 2] for n in range(0, 8, 2))
    grad_ref, feed_ref, start_ref, sems = refs[8:]
    _, rows, columns = grad_ref.shape
    half = rows // 2
    width = columns // CHIPS
    steps = columns // CHUNK
    seed = seed_ref[0]
    first = lax.axis_index("z") * columns
    core = lax.axis_index("core")
    copies = []
    for j in range(steps):
        pair = (
            pltpu.make_async_copy(grad_hbm.at[:, :, cols(j)], grad_ref.at[:, :, cols(j)], sems.at[j, 0]),
            pltpu.make_async_copy(feed_hbm.at[:, :, cols(j)], feed_ref.at[:, :, cols(j)], sems.at[j, 1]),
        )
        for copy in pair:
            copy.start()
        copies.append(pair)
    for left_ref in lefts:
        left_ref[rows:, :] = jnp.zeros((left_ref.shape[0] - rows, RANK), f32)
    for j in range(steps):
        high, low = split(start_block(seed, first + j * CHUNK, CHUNK))
        start_ref[cols(j), :RANK] = high
        start_ref[cols(j), RANK:] = low
    saves = []
    for j in range(steps):
        for copy in copies[j]:
            copy.wait()
        both = start_ref[cols(j), :]
        for slot in range(2):
            m = core ^ slot
            summed = grad_ref[m, :, cols(j)].astype(f32) + feed_ref[m, :, cols(j)]
            if slot:
                sums[slot][:, cols(j)] = summed
            else:
                feed_ref[m, :, cols(j)] = summed
                save = pltpu.make_async_copy(feed_ref.at[m, :, cols(j)], sums[slot].at[:, cols(j)], sems.at[j, 2])
                save.start()
                saves.append(save)
            for tile in range(CHIPS):
                begin = tile * width
                end = min(begin + LANES, columns)
                if (end - 1) // CHUNK != j:
                    continue
                block = sums[slot][:, begin:end] if slot else feed_ref[m, :, begin:end]
                if end - begin < LANES:
                    block = jnp.concatenate([block, jnp.zeros((rows, LANES - end + begin), f32)], axis=1)
                upper, lower = places(tile)
                uppers[slot][upper] = block[:half]
                lowers[slot][lower] = block[half:]
            s_high, s_low = split(summed)
            wide = dot(s_high, both)
            piece = wide[:, :RANK] + wide[:, RANK:] + dot(s_low, both[:, :RANK])
            if j == 0:
                lefts[slot][:rows, :] = piece
            else:
                lefts[slot][:rows, :] += piece
    for save in saves:
        save.wait()


def eliminate(gram):
    lane = lax.broadcasted_iota(jnp.int32, (1, RANK), 1)
    count = RANK // GROUP
    blocks = [gram[GROUP * b : GROUP * (b + 1), :] for b in range(count)]
    sub = lax.broadcasted_iota(jnp.int32, (GROUP, RANK), 0)
    pivots = []
    for b in range(count):
        start = GROUP * b
        panel = blocks[b]
        spread_cols = [jnp.broadcast_to(panel[:, start + t : start + t + 1], (GROUP, RANK)) for t in range(GROUP)]
        a = [[spread_cols[t][s : s + 1, :] for t in range(GROUP)] for s in range(GROUP)]
        factors = [[None] * GROUP for _ in range(GROUP)]
        inverses = []
        for t in range(GROUP):
            pivots.append(a[t][t])
            inverses.append(1.0 / a[t][t])
            for s in range(t + 1, GROUP):
                factors[s][t] = a[s][t] * inverses[t]
                for u in range(t + 1, GROUP):
                    a[s][u] = a[s][u] - factors[s][t] * a[t][u]
        rows, sources = [], []
        for s in range(GROUP):
            row = panel[s : s + 1, :]
            for t in range(s):
                row = jnp.where(lane == start + t, 0.0, row) - factors[s][t] * sources[t]
            rows.append(row)
            sources.append(jnp.where(lane == start + s, 1.0, row))
        for s in range(GROUP):
            panel = jnp.where(sub == s, rows[s], panel)
        blocks[b] = panel
        for later in range(b + 1, count):
            block = blocks[later]
            heads = [jnp.broadcast_to(block[:, start + t : start + t + 1], (GROUP, RANK)) for t in range(GROUP)]
            for t in range(GROUP):
                factor = heads[t] * inverses[t]
                for u in range(t + 1, GROUP):
                    heads[u] = heads[u] - factor * a[t][u]
                block = jnp.where(lane == start + t, 0.0, block) - factor * sources[t]
            blocks[later] = block
    return jnp.concatenate(blocks, axis=0), jnp.concatenate(pivots, axis=0)


def basis_kernel(left_ref, after_ref, basis_ref):
    del after_ref
    left = left_ref[: basis_ref.shape[0], :] * (1.0 / 32)
    lower, pivots = eliminate(exact_dot(left, left, ((0,), (0,))))
    i = lax.broadcasted_iota(jnp.int32, (RANK, RANK), 0)
    j = lax.broadcasted_iota(jnp.int32, (RANK, RANK), 1)
    inverse = jnp.where(i > j, lower, jnp.where(i == j, 1.0, 0.0)) * lax.rsqrt(pivots)
    basis_ref[...] = exact_dot(left, inverse, ((1,), (1,)))


def sum_kernel(part_ref, out_ref):
    total = part_ref[0]
    for i in range(1, part_ref.shape[0]):
        total = total + part_ref[i]
    for i in range(out_ref.shape[0]):
        out_ref[i] = total


def sum_spread(parts, count):
    return pl.pallas_call(
        sum_kernel,
        in_specs=[vmem],
        out_specs=vmem,
        out_shape=pltpu.VMEM((count,) + parts.shape[1:], f32),
        compiler_params=params(4),
        name="sum_spread",
    )(parts)


def halve_kernel(after_ref, *refs):
    del after_ref
    for side in range(2):
        kept_ref, got_ref = refs[2 * side : 2 * side + 2]
        keep_ref, send_ref = refs[4 + 2 * side : 6 + 2 * side]
        count = keep_ref.shape[0]
        for i in range(count):
            keep_ref[i] = kept_ref[i] + got_ref[i]
            send_ref[i] = kept_ref[count + i] + got_ref[count + i]


def halve(after, *blocks):
    shape = (blocks[0].shape[0] // 2,) + blocks[0].shape[1:]
    return pl.pallas_call(
        halve_kernel,
        in_specs=[hbm] + [vmem] * 4,
        out_specs=[vmem] * 4,
        out_shape=[pltpu.VMEM(shape, f32)] * 4,
        compiler_params=params(4),
        name="halve",
    )(after, *blocks)


def join_kernel(after_ref, upper_ref, upper_got_ref, lower_ref, lower_got_ref, out_ref):
    del after_ref
    half = upper_ref.shape[1]
    for i in range(out_ref.shape[0]):
        out_ref[i, :half, :] = upper_ref[i] + upper_got_ref[i]
        out_ref[i, half:, :] = lower_ref[i] + lower_got_ref[i]


def finish_kernel(part_ref, basis_ref, out_ref):
    total = part_ref[0]
    for i in range(1, part_ref.shape[0]):
        total = total + part_ref[i]
    right = exact_dot(total * (1.0 / 32), basis_ref[...], ((0,), (0,)))
    for i in range(out_ref.shape[0]):
        out_ref[i] = right[: out_ref.shape[1], :]


def update_kernel(slot, basis_ref, right_ref, sum_ref, *rest):
    out_hbm, right_hbm, basis_hbm, out_ref, sems = rest[3 * slot :]
    columns = sum_ref.shape[1]
    steps = columns // CHUNK
    m = lax.axis_index("core") ^ slot
    stores = [
        pltpu.make_async_copy(right_ref, right_hbm.at[m], sems.at[steps]),
        pltpu.make_async_copy(basis_ref, basis_hbm.at[m], sems.at[steps + 1]),
    ]
    for copy in stores:
        copy.start()
    high, low = split(basis_ref[...])
    wide = jnp.concatenate([high, low], axis=1)
    for j in range(steps):
        r_high, r_low = split(right_ref[cols(j), :])
        rebuilt = dot(wide, jnp.concatenate([r_high, r_high], axis=1), ((1,), (1,)))
        rebuilt = rebuilt + dot(high, r_low, ((1,), (1,)))
        out_ref[:, cols(j)] = sum_ref[:, cols(j)] - rebuilt
        copy = pltpu.make_async_copy(out_ref.at[:, cols(j)], out_hbm.at[m, :, cols(j)], sems.at[j])
        copy.start()
        stores.append(copy)
    for copy in stores:
        copy.wait()


def update(slot, basis, right, summed, previous=()):
    rows, columns = summed.shape
    return pl.pallas_call(
        functools.partial(update_kernel, slot),
        in_specs=[vmem] * 3 + [hbm] * len(previous),
        out_specs=[hbm] * 3,
        out_shape=[
            jax.ShapeDtypeStruct((2, rows, columns), f32),
            jax.ShapeDtypeStruct((2, columns, RANK), f32),
            jax.ShapeDtypeStruct((2, rows, RANK), f32),
        ],
        scratch_shapes=[
            pltpu.VMEM((rows, columns), f32),
            pltpu.SemaphoreType.DMA((2 + columns // CHUNK,)),
        ],
        input_output_aliases={3: 0, 4: 1, 5: 2} if previous else {},
        cost_estimate=pl.CostEstimate(
            flops=6 * rows * columns * RANK, bytes_accessed=8 * rows * columns, transcendentals=0
        ),
        compiler_params=params(8),
        name=("update_mine", "update_other")[slot],
    )(basis, right, summed, *previous)


def swap(x):
    return lax.ppermute(x, "core", [(0, 1), (1, 0)])


def cross(x, axis):
    return lax.ppermute(x, (axis + "h", axis + "l"), [(i, 3 - i) for i in range(4)])


def exchange(x, axes=PLANE):
    return lax.all_to_all(x, axes, 0, 0)


def on_device(gradients, feedback, seed_value):
    gradients = pltpu.with_memory_space_constraint(gradients[0], pltpu.HBM)
    feedback = pltpu.with_memory_space_constraint(feedback[0], pltpu.HBM)
    mats, rows, columns = gradients.shape
    depth = lax.axis_size("z")
    share = -(-rows // (CHIPS * TILE)) * TILE
    padded = CHIPS * share

    mine, other, upper, upper_other, lower, lower_other, summed, summed_other = pl.pallas_call(
        left_kernel,
        in_specs=[smem, hbm, hbm],
        out_specs=[vmem] * 6 + [hbm, vmem],
        out_shape=[pltpu.VMEM((padded, RANK), f32)] * 2
        + [pltpu.VMEM((CHIPS, rows // 2, LANES), f32)] * 4
        + [pltpu.HBM((rows, columns), f32), pltpu.VMEM((rows, columns), f32)],
        scratch_shapes=[
            pltpu.VMEM((mats, rows, columns), bf16),
            pltpu.VMEM((mats, rows, columns), f32),
            pltpu.VMEM((columns, 2 * RANK), bf16),
            pltpu.SemaphoreType.DMA((columns // CHUNK, 4)),
        ],
        compiler_params=params(20),
        name="left_part",
    )(seed_value, gradients, feedback)

    left = mine + swap(other)
    left, upper_other, lower_other = lax.optimization_barrier((left, upper_other, lower_other))
    upper_got, lower_got = swap(upper_other), swap(lower_other)
    left = exchange(left.reshape(CHIPS, share, RANK))
    upper, upper_send, lower, lower_send = halve(left, upper, upper_got, lower, lower_got)
    upper_got, lower_got = cross(upper_send, "x"), cross(lower_send, "y")
    left = exchange(sum_spread(left, depth), "z")
    upper, upper_send, lower, lower_send = halve(left, upper, upper_got, lower, lower_got)
    upper_got, lower_got = cross(upper_send, "y"), cross(lower_send, "x")
    left = exchange(sum_spread(left, CHIPS))

    quarter = pl.pallas_call(
        join_kernel,
        in_specs=[hbm] + [vmem] * 4,
        out_specs=vmem,
        out_shape=pltpu.VMEM((CHIPS // 4, rows, LANES), f32),
        compiler_params=params(4),
        name="join",
    )(left, upper, upper_got, lower, lower_got)
    basis = pl.pallas_call(
        basis_kernel,
        in_specs=[vmem, hbm],
        out_specs=vmem,
        out_shape=pltpu.VMEM((rows, RANK), f32),
        cost_estimate=pl.CostEstimate(flops=5_000_000_000, bytes_accessed=400_000, transcendentals=0),
        compiler_params=params(8),
        name="basis",
    )(left.reshape(padded, RANK), quarter)
    basis_other = swap(basis)
    right = pl.pallas_call(
        finish_kernel,
        in_specs=[vmem, vmem],
        out_specs=vmem,
        out_shape=pltpu.VMEM((CHIPS, columns // CHIPS, RANK), f32),
        compiler_params=params(4),
        name="finish",
    )(exchange(quarter, ("xl", "yl")), basis)
    right = exchange(right).reshape(columns, RANK)
    right_other = swap(right)

    outs = update(0, basis, right, summed)
    new_feedback, right_factor, left_basis = update(1, basis_other, right_other, summed_other, outs)
    return new_feedback[None], left_basis, right_factor


def solution(mesh):
    fine = Mesh(mesh.devices.reshape(2, 2, 2, 2, 2, -1), PLANE + ("core", "z"))
    dp = PLANE + ("core",)
    placed = (P(dp, None, None, "z"), P(dp, None, None, "z"), P())
    return jax.shard_map(
        on_device,
        mesh=fine,
        in_specs=placed,
        out_specs=(P(dp, None, None, "z"), P(), P(None, "z", None)),
        check_vma=False,
    )
```

```python
import functools

import jax
import jax.numpy as jnp
from jax import lax
from jax.experimental import pallas as pl
from jax.experimental.pallas import tpu as pltpu
from jax.sharding import Mesh, PartitionSpec as P

RANK = 128
PRIME = 32749
CHIPS = 16
CHUNK = 256
LANES = 128
GROUP = 8
TILE = 8
MIB = 1024 * 1024

unit_scale = 3.4641016
f32 = jnp.float32
bf16 = jnp.bfloat16

smem = pl.BlockSpec(memory_space=pltpu.SMEM)
hbm = pl.BlockSpec(memory_space=pltpu.HBM)
vmem = pl.BlockSpec(memory_space=pltpu.VMEM)

PLANE = ("xh", "xl", "yh", "yl")


def split(x):
    high = x.astype(bf16)
    return high, (x - high.astype(f32)).astype(bf16)


def dot(a, b, contract=((1,), (0,))):
    return lax.dot_general(a, b, (contract, ((), ())), preferred_element_type=f32)


def exact_dot(a, b, contract):
    return lax.dot_general(
        a, b, (contract, ((), ())), precision=lax.Precision.HIGHEST, preferred_element_type=f32
    )


def cols(j):
    return pl.ds(j * CHUNK, CHUNK)


def params(mib):
    return pltpu.CompilerParams(vmem_limit_bytes=mib * MIB)


def centred(x):
    quotient = (x.astype(f32) * (1.0 / PRIME) + 0.5).astype(jnp.int32)
    return x - quotient * PRIME


def first_hash(columns):
    i = lax.broadcasted_iota(jnp.int32, (columns, RANK), 0)
    rank = lax.broadcasted_iota(jnp.int32, (columns, RANK), 1)
    return centred(i * 131 + rank * 977)


def start_block(hashed, seed, first):
    columns = hashed.shape[0]
    col = first + lax.broadcasted_iota(jnp.int32, (columns, RANK), 0)
    rank = lax.broadcasted_iota(jnp.int32, (1, RANK), 1)
    hashed = hashed + centred(first * 131 + seed)
    hashed = centred(hashed * hashed + (rank * 17 + 7))
    hashed = centred(hashed * hashed + col)
    return hashed.astype(f32) * (unit_scale / PRIME) + jnp.where(hashed < 0, 0.5 * unit_scale, -0.5 * unit_scale)


def places(tile):
    xh, xl, yh, yl = tile >> 3, (tile >> 2) & 1, (tile >> 1) & 1, tile & 1
    rest = 2 * xl + yl
    far_x, far_y = xh ^ lax.axis_index("xh"), yh ^ lax.axis_index("yh")
    return 8 * far_x + 4 * far_y + rest, 8 * far_y + 4 * far_x + rest


def left_kernel(seed_ref, grad_hbm, feed_hbm, *refs):
    lefts, uppers, lowers, sums = (refs[n : n + 2] for n in range(0, 8, 2))
    grad_ref, feed_ref, start_ref, sems = refs[8:]
    _, rows, columns = grad_ref.shape
    half = rows // 2
    width = columns // CHIPS
    steps = columns // CHUNK
    seed = seed_ref[0]
    first = lax.axis_index("z") * columns
    core = lax.axis_index("core")
    copies = []
    for j in range(steps):
        pair = (
            pltpu.make_async_copy(grad_hbm.at[:, :, cols(j)], grad_ref.at[:, :, cols(j)], sems.at[j, 0]),
            pltpu.make_async_copy(feed_hbm.at[:, :, cols(j)], feed_ref.at[:, :, cols(j)], sems.at[j, 1]),
        )
        for copy in pair:
            copy.start()
        copies.append(pair)
    for left_ref in lefts:
        left_ref[rows:, :] = jnp.zeros((left_ref.shape[0] - rows, RANK), f32)
    hashed = first_hash(CHUNK)
    for j in range(steps):
        high, low = split(start_block(hashed, seed, first + j * CHUNK))
        start_ref[cols(j), :RANK] = high
        start_ref[cols(j), RANK:] = low
    saves = []
    for j in range(steps):
        for copy in copies[j]:
            copy.wait()
        both = start_ref[cols(j), :]
        for slot in range(2):
            m = core ^ slot
            summed = grad_ref[m, :, cols(j)].astype(f32) + feed_ref[m, :, cols(j)]
            if slot:
                sums[slot][:, cols(j)] = summed
            else:
                feed_ref[m, :, cols(j)] = summed
                save = pltpu.make_async_copy(feed_ref.at[m, :, cols(j)], sums[slot].at[:, cols(j)], sems.at[j, 2])
                save.start()
                saves.append(save)
            for tile in range(CHIPS):
                begin = tile * width
                end = min(begin + LANES, columns)
                if (end - 1) // CHUNK != j:
                    continue
                block = sums[slot][:, begin:end] if slot else feed_ref[m, :, begin:end]
                if end - begin < LANES:
                    block = jnp.concatenate([block, jnp.zeros((rows, LANES - end + begin), f32)], axis=1)
                upper, lower = places(tile)
                uppers[slot][upper] = block[:half]
                lowers[slot][lower] = block[half:]
            s_high, s_low = split(summed)
            wide = dot(s_high, both)
            piece = wide[:, :RANK] + wide[:, RANK:] + dot(s_low, both[:, :RANK])
            if j == 0:
                lefts[slot][:rows, :] = piece
            else:
                lefts[slot][:rows, :] += piece
    for save in saves:
        save.wait()


def eliminate(gram):
    lane = lax.broadcasted_iota(jnp.int32, (1, RANK), 1)
    count = RANK // GROUP
    blocks = [gram[GROUP * b : GROUP * (b + 1), :] for b in range(count)]
    sub = lax.broadcasted_iota(jnp.int32, (GROUP, RANK), 0)
    pivots = []
    for b in range(count):
        start = GROUP * b
        panel = blocks[b]
        spread_cols = [jnp.broadcast_to(panel[:, start + t : start + t + 1], (GROUP, RANK)) for t in range(GROUP)]
        a = [[spread_cols[t][s : s + 1, :] for t in range(GROUP)] for s in range(GROUP)]
        factors = [[None] * GROUP for _ in range(GROUP)]
        inverses = []
        for t in range(GROUP):
            pivots.append(a[t][t])
            inverses.append(1.0 / a[t][t])
            for s in range(t + 1, GROUP):
                factors[s][t] = a[s][t] * inverses[t]
                for u in range(t + 1, GROUP):
                    a[s][u] = a[s][u] - factors[s][t] * a[t][u]
        rows, sources = [], []
        for s in range(GROUP):
            row = panel[s : s + 1, :]
            for t in range(s):
                row = jnp.where(lane == start + t, 0.0, row) - factors[s][t] * sources[t]
            rows.append(row)
            sources.append(jnp.where(lane == start + s, 1.0, row))
        for s in range(GROUP):
            panel = jnp.where(sub == s, rows[s], panel)
        blocks[b] = panel
        for later in range(b + 1, count):
            block = blocks[later]
            heads = [jnp.broadcast_to(block[:, start + t : start + t + 1], (GROUP, RANK)) for t in range(GROUP)]
            for t in range(GROUP):
                factor = heads[t] * inverses[t]
                for u in range(t + 1, GROUP):
                    heads[u] = heads[u] - factor * a[t][u]
                block = jnp.where(lane == start + t, 0.0, block) - factor * sources[t]
            blocks[later] = block
    return jnp.concatenate(blocks, axis=0), jnp.concatenate(pivots, axis=0)


def basis_kernel(left_ref, after_ref, basis_ref):
    del after_ref
    left = left_ref[: basis_ref.shape[0], :] * (1.0 / 32)
    lower, pivots = eliminate(exact_dot(left, left, ((0,), (0,))))
    i = lax.broadcasted_iota(jnp.int32, (RANK, RANK), 0)
    j = lax.broadcasted_iota(jnp.int32, (RANK, RANK), 1)
    inverse = jnp.where(i > j, lower, jnp.where(i == j, 1.0, 0.0)) * lax.rsqrt(pivots)
    basis_ref[...] = exact_dot(left, inverse, ((1,), (1,)))


def sum_kernel(part_ref, out_ref):
    total = part_ref[0]
    for i in range(1, part_ref.shape[0]):
        total = total + part_ref[i]
    for i in range(out_ref.shape[0]):
        out_ref[i] = total


def sum_spread(parts, count):
    return pl.pallas_call(
        sum_kernel,
        in_specs=[vmem],
        out_specs=vmem,
        out_shape=pltpu.VMEM((count,) + parts.shape[1:], f32),
        compiler_params=params(4),
        name="sum_spread",
    )(parts)


def halve_kernel(after_ref, *refs):
    del after_ref
    for side in range(2):
        kept_ref, got_ref = refs[2 * side : 2 * side + 2]
        keep_ref, send_ref = refs[4 + 2 * side : 6 + 2 * side]
        count = keep_ref.shape[0]
        for i in range(count):
            keep_ref[i] = kept_ref[i] + got_ref[i]
            send_ref[i] = kept_ref[count + i] + got_ref[count + i]


def halve(after, *blocks):
    shape = (blocks[0].shape[0] // 2,) + blocks[0].shape[1:]
    return pl.pallas_call(
        halve_kernel,
        in_specs=[hbm] + [vmem] * 4,
        out_specs=[vmem] * 4,
        out_shape=[pltpu.VMEM(shape, f32)] * 4,
        compiler_params=params(4),
        name="halve",
    )(after, *blocks)


def join_kernel(after_ref, upper_ref, upper_got_ref, lower_ref, lower_got_ref, out_hbm, out_ref, sems):
    del after_ref
    half = upper_ref.shape[1]
    copies = []
    for i in range(out_ref.shape[0]):
        out_ref[i, :half, :] = upper_ref[i] + upper_got_ref[i]
        out_ref[i, half:, :] = lower_ref[i] + lower_got_ref[i]
        copies.append(pltpu.make_async_copy(out_ref.at[i], out_hbm.at[i], sems.at[i]))
        copies[i].start()
    for copy in copies:
        copy.wait()


def finish_kernel(part_ref, basis_ref, out_ref):
    total = part_ref[0]
    for i in range(1, part_ref.shape[0]):
        total = total + part_ref[i]
    high, low = split(total * (1.0 / 32))
    b_high, b_low = split(basis_ref[...])
    rows = ((0,), (0,))
    wide = dot(high, jnp.concatenate([b_high, b_low], axis=1), rows)
    right = wide[:, :RANK] + wide[:, RANK:] + dot(low, b_high, rows)
    for i in range(out_ref.shape[0]):
        out_ref[i] = right[: out_ref.shape[1], :]


def update_kernel(slot, basis_ref, right_ref, sum_ref, *rest):
    out_hbm, right_hbm, basis_hbm, out_ref, sems = rest[3 * slot :]
    columns = sum_ref.shape[1]
    steps = columns // CHUNK
    m = lax.axis_index("core") ^ slot
    stores = [
        pltpu.make_async_copy(right_ref, right_hbm.at[m], sems.at[steps]),
        pltpu.make_async_copy(basis_ref, basis_hbm.at[m], sems.at[steps + 1]),
    ]
    for copy in stores:
        copy.start()
    high, low = split(basis_ref[...])
    wide = jnp.concatenate([high, low], axis=1)
    for j in range(steps):
        r_high, r_low = split(right_ref[cols(j), :])
        rebuilt = dot(wide, jnp.concatenate([r_high, r_high], axis=1), ((1,), (1,)))
        rebuilt = rebuilt + dot(high, r_low, ((1,), (1,)))
        out_ref[:, cols(j)] = sum_ref[:, cols(j)] - rebuilt
        copy = pltpu.make_async_copy(out_ref.at[:, cols(j)], out_hbm.at[m, :, cols(j)], sems.at[j])
        copy.start()
        stores.append(copy)
    for copy in stores:
        copy.wait()


def update(slot, basis, right, summed, previous=()):
    rows, columns = summed.shape
    return pl.pallas_call(
        functools.partial(update_kernel, slot),
        in_specs=[vmem] * 3 + [hbm] * len(previous),
        out_specs=[hbm] * 3,
        out_shape=[
            jax.ShapeDtypeStruct((2, rows, columns), f32),
            jax.ShapeDtypeStruct((2, columns, RANK), f32),
            jax.ShapeDtypeStruct((2, rows, RANK), f32),
        ],
        scratch_shapes=[
            pltpu.VMEM((rows, columns), f32),
            pltpu.SemaphoreType.DMA((2 + columns // CHUNK,)),
        ],
        input_output_aliases={3: 0, 4: 1, 5: 2} if previous else {},
        cost_estimate=pl.CostEstimate(
            flops=6 * rows * columns * RANK, bytes_accessed=8 * rows * columns, transcendentals=0
        ),
        compiler_params=params(8),
        name=("update_mine", "update_other")[slot],
    )(basis, right, summed, *previous)


def swap(x):
    return lax.ppermute(x, "core", [(0, 1), (1, 0)])


def cross(x, axis):
    return lax.ppermute(x, (axis + "h", axis + "l"), [(i, 3 - i) for i in range(4)])


def exchange(x, axes=PLANE):
    return lax.all_to_all(x, axes, 0, 0)


def on_device(gradients, feedback, seed_value):
    gradients = pltpu.with_memory_space_constraint(gradients[0], pltpu.HBM)
    feedback = pltpu.with_memory_space_constraint(feedback[0], pltpu.HBM)
    mats, rows, columns = gradients.shape
    depth = lax.axis_size("z")
    share = -(-rows // (CHIPS * TILE)) * TILE
    padded = CHIPS * share

    mine, other, upper, upper_other, lower, lower_other, summed, summed_other = pl.pallas_call(
        left_kernel,
        in_specs=[smem, hbm, hbm],
        out_specs=[vmem] * 6 + [hbm, vmem],
        out_shape=[pltpu.VMEM((padded, RANK), f32)] * 2
        + [pltpu.VMEM((CHIPS, rows // 2, LANES), f32)] * 4
        + [pltpu.HBM((rows, columns), f32), pltpu.VMEM((rows, columns), f32)],
        scratch_shapes=[
            pltpu.VMEM((mats, rows, columns), bf16),
            pltpu.VMEM((mats, rows, columns), f32),
            pltpu.VMEM((columns, 2 * RANK), bf16),
            pltpu.SemaphoreType.DMA((columns // CHUNK, 4)),
        ],
        compiler_params=params(20),
        name="left_part",
    )(seed_value, gradients, feedback)

    left = mine + swap(other)
    left, upper_other, lower_other = lax.optimization_barrier((left, upper_other, lower_other))
    upper_got, lower_got = swap(upper_other), swap(lower_other)
    left = exchange(left.reshape(CHIPS, share, RANK))
    upper, upper_send, lower, lower_send = halve(left, upper, upper_got, lower, lower_got)
    upper_got, lower_got = cross(upper_send, "x"), cross(lower_send, "y")
    left = exchange(sum_spread(left, depth), "z")
    upper, upper_send, lower, lower_send = halve(left, upper, upper_got, lower, lower_got)
    upper_got, lower_got = cross(upper_send, "y"), cross(lower_send, "x")
    left = exchange(sum_spread(left, CHIPS))

    quarter = pl.pallas_call(
        join_kernel,
        in_specs=[hbm] + [vmem] * 4,
        out_specs=hbm,
        out_shape=pltpu.HBM((CHIPS // 4, rows, LANES), f32),
        scratch_shapes=[pltpu.VMEM((CHIPS // 4, rows, LANES), f32), pltpu.SemaphoreType.DMA((CHIPS // 4,))],
        compiler_params=params(4),
        name="join",
    )(left, upper, upper_got, lower, lower_got)
    basis = pl.pallas_call(
        basis_kernel,
        in_specs=[vmem, hbm],
        out_specs=vmem,
        out_shape=pltpu.VMEM((rows, RANK), f32),
        cost_estimate=pl.CostEstimate(flops=5_000_000_000, bytes_accessed=400_000, transcendentals=0),
        compiler_params=params(8),
        name="basis",
    )(left.reshape(padded, RANK), quarter)
    basis_other = swap(basis)
    right = pl.pallas_call(
        finish_kernel,
        in_specs=[vmem, vmem],
        out_specs=vmem,
        out_shape=pltpu.VMEM((CHIPS, columns // CHIPS, RANK), f32),
        compiler_params=params(4),
        name="finish",
    )(exchange(quarter, ("xl", "yl")), basis)
    right = exchange(right).reshape(columns, RANK)
    right_other = swap(right)

    outs = update(0, basis, right, summed)
    new_feedback, right_factor, left_basis = update(1, basis_other, right_other, summed_other, outs)
    return new_feedback[None], left_basis, right_factor


def solution(mesh):
    fine = Mesh(mesh.devices.reshape(2, 2, 2, 2, 2, -1), PLANE + ("core", "z"))
    dp = PLANE + ("core",)
    placed = (P(dp, None, None, "z"), P(dp, None, None, "z"), P())
    return jax.shard_map(
        on_device,
        mesh=fine,
        in_specs=placed,
        out_specs=(P(dp, None, None, "z"), P(), P(None, "z", None)),
        check_vma=False,
    )
```

```python
import functools

import jax
import jax.numpy as jnp
from jax import lax
from jax.experimental import pallas as pl
from jax.experimental.pallas import tpu as pltpu
from jax.sharding import Mesh, PartitionSpec as P

RANK = 128
PRIME = 32749
CHIPS = 16
CHUNK = 256
LANES = 128
GROUP = 8
TILE = 8
MIB = 1024 * 1024

unit_scale = 3.4641016
f32 = jnp.float32
bf16 = jnp.bfloat16

smem = pl.BlockSpec(memory_space=pltpu.SMEM)
hbm = pl.BlockSpec(memory_space=pltpu.HBM)
vmem = pl.BlockSpec(memory_space=pltpu.VMEM)

PLANE = ("xh", "xl", "yh", "yl")


def split(x):
    high = x.astype(bf16)
    return high, (x - high.astype(f32)).astype(bf16)


def dot(a, b, contract=((1,), (0,))):
    return lax.dot_general(a, b, (contract, ((), ())), preferred_element_type=f32)


def exact_dot(a, b, contract):
    return lax.dot_general(
        a, b, (contract, ((), ())), precision=lax.Precision.HIGHEST, preferred_element_type=f32
    )


def cols(j):
    return pl.ds(j * CHUNK, CHUNK)


def params(mib):
    return pltpu.CompilerParams(vmem_limit_bytes=mib * MIB)


def centred(x):
    quotient = (x.astype(f32) * (1.0 / PRIME) + 0.5).astype(jnp.int32)
    return x - quotient * PRIME


def first_hash(columns):
    i = lax.broadcasted_iota(jnp.int32, (columns, RANK), 0)
    rank = lax.broadcasted_iota(jnp.int32, (columns, RANK), 1)
    return centred(i * 131 + rank * 977)


def start_block(hashed, seed, first):
    columns = hashed.shape[0]
    col = first + lax.broadcasted_iota(jnp.int32, (columns, RANK), 0)
    rank = lax.broadcasted_iota(jnp.int32, (1, RANK), 1)
    hashed = hashed + centred(first * 131 + seed)
    hashed = centred(hashed * hashed + (rank * 17 + 7))
    hashed = centred(hashed * hashed + col)
    return hashed.astype(f32) * (unit_scale / PRIME) + jnp.where(hashed < 0, 0.5 * unit_scale, -0.5 * unit_scale)


def places(tile):
    xh, xl, yh, yl = tile >> 3, (tile >> 2) & 1, (tile >> 1) & 1, tile & 1
    rest = 2 * xl + yl
    far_x, far_y = xh ^ lax.axis_index("xh"), yh ^ lax.axis_index("yh")
    return 8 * far_x + 4 * far_y + rest, 8 * far_y + 4 * far_x + rest


def left_kernel(seed_ref, grad_hbm, feed_hbm, *refs):
    lefts, (upper_ref, lower_ref, tiles_ref), sums = refs[:2], refs[2:5], refs[5:7]
    grad_ref, feed_ref, start_ref, sems = refs[7:]
    _, rows, columns = grad_ref.shape
    half = rows // 2
    width = columns // CHIPS
    steps = columns // CHUNK
    seed = seed_ref[0]
    first = lax.axis_index("z") * columns
    core = lax.axis_index("core")
    copies = []
    for j in range(steps):
        pair = (
            pltpu.make_async_copy(grad_hbm.at[:, :, cols(j)], grad_ref.at[:, :, cols(j)], sems.at[j, 0]),
            pltpu.make_async_copy(feed_hbm.at[:, :, cols(j)], feed_ref.at[:, :, cols(j)], sems.at[j, 1]),
        )
        for copy in pair:
            copy.start()
        copies.append(pair)
    for left_ref in lefts:
        left_ref[rows:, :] = jnp.zeros((left_ref.shape[0] - rows, RANK), f32)
    hashed = first_hash(CHUNK)
    for j in range(steps):
        high, low = split(start_block(hashed, seed, first + j * CHUNK))
        start_ref[cols(j), :RANK] = high
        start_ref[cols(j), RANK:] = low
    saves = []
    for j in range(steps):
        for copy in copies[j]:
            copy.wait()
        both = start_ref[cols(j), :]
        for slot in range(2):
            m = core ^ slot
            summed = grad_ref[m, :, cols(j)].astype(f32) + feed_ref[m, :, cols(j)]
            if slot:
                sums[slot][:, cols(j)] = summed
            else:
                feed_ref[m, :, cols(j)] = summed
                save = pltpu.make_async_copy(feed_ref.at[m, :, cols(j)], sums[slot].at[:, cols(j)], sems.at[j, 2])
                save.start()
                saves.append(save)
            for tile in range(CHIPS):
                begin = tile * width
                end = min(begin + LANES, columns)
                if (end - 1) // CHUNK != j:
                    continue
                block = sums[slot][:, begin:end] if slot else feed_ref[m, :, begin:end]
                if end - begin < LANES:
                    block = jnp.concatenate([block, jnp.zeros((rows, LANES - end + begin), f32)], axis=1)
                upper, lower = places(tile)
                if slot:
                    tiles_ref[upper, :half, :] = block[:half]
                    tiles_ref[lower, half:, :] = block[half:]
                else:
                    upper_ref[upper] = block[:half]
                    lower_ref[lower] = block[half:]
            s_high, s_low = split(summed)
            wide = dot(s_high, both)
            piece = wide[:, :RANK] + wide[:, RANK:] + dot(s_low, both[:, :RANK])
            if j == 0:
                lefts[slot][:rows, :] = piece
            else:
                lefts[slot][:rows, :] += piece
    for save in saves:
        save.wait()


def eliminate(gram):
    lane = lax.broadcasted_iota(jnp.int32, (1, RANK), 1)
    count = RANK // GROUP
    blocks = [gram[GROUP * b : GROUP * (b + 1), :] for b in range(count)]
    sub = lax.broadcasted_iota(jnp.int32, (GROUP, RANK), 0)
    pivots = []
    for b in range(count):
        start = GROUP * b
        panel = blocks[b]
        spread_cols = [jnp.broadcast_to(panel[:, start + t : start + t + 1], (GROUP, RANK)) for t in range(GROUP)]
        a = [[spread_cols[t][s : s + 1, :] for t in range(GROUP)] for s in range(GROUP)]
        factors = [[None] * GROUP for _ in range(GROUP)]
        inverses = []
        for t in range(GROUP):
            pivots.append(a[t][t])
            inverses.append(1.0 / a[t][t])
            for s in range(t + 1, GROUP):
                factors[s][t] = a[s][t] * inverses[t]
                for u in range(t + 1, GROUP):
                    a[s][u] = a[s][u] - factors[s][t] * a[t][u]
        rows, sources = [], []
        for s in range(GROUP):
            row = panel[s : s + 1, :]
            for t in range(s):
                row = jnp.where(lane == start + t, 0.0, row) - factors[s][t] * sources[t]
            rows.append(row)
            sources.append(jnp.where(lane == start + s, 1.0, row))
        for s in range(GROUP):
            panel = jnp.where(sub == s, rows[s], panel)
        blocks[b] = panel
        for later in range(b + 1, count):
            block = blocks[later]
            heads = [jnp.broadcast_to(block[:, start + t : start + t + 1], (GROUP, RANK)) for t in range(GROUP)]
            for t in range(GROUP):
                factor = heads[t] * inverses[t]
                for u in range(t + 1, GROUP):
                    heads[u] = heads[u] - factor * a[t][u]
                block = jnp.where(lane == start + t, 0.0, block) - factor * sources[t]
            blocks[later] = block
    return jnp.concatenate(blocks, axis=0), jnp.concatenate(pivots, axis=0)


def basis_kernel(left_ref, after_ref, basis_ref):
    del after_ref
    left = left_ref[: basis_ref.shape[0], :] * (1.0 / 32)
    lower, pivots = eliminate(exact_dot(left, left, ((0,), (0,))))
    i = lax.broadcasted_iota(jnp.int32, (RANK, RANK), 0)
    j = lax.broadcasted_iota(jnp.int32, (RANK, RANK), 1)
    inverse = jnp.where(i > j, lower, jnp.where(i == j, 1.0, 0.0)) * lax.rsqrt(pivots)
    basis_ref[...] = exact_dot(left, inverse, ((1,), (1,)))


def sum_kernel(part_ref, out_ref):
    total = part_ref[0]
    for i in range(1, part_ref.shape[0]):
        total = total + part_ref[i]
    for i in range(out_ref.shape[0]):
        out_ref[i] = total


def sum_spread(parts, count):
    return pl.pallas_call(
        sum_kernel,
        in_specs=[vmem],
        out_specs=vmem,
        out_shape=pltpu.VMEM((count,) + parts.shape[1:], f32),
        compiler_params=params(4),
        name="sum_spread",
    )(parts)


def halve_kernel(after_ref, *refs):
    del after_ref
    for side in range(2):
        kept_ref, got_ref = refs[2 * side : 2 * side + 2]
        keep_ref, send_ref = refs[4 + 2 * side : 6 + 2 * side]
        count = keep_ref.shape[0]
        for i in range(count):
            keep_ref[i] = kept_ref[i] + got_ref[i]
            send_ref[i] = kept_ref[count + i] + got_ref[count + i]


def first_halve_kernel(after_ref, upper_ref, lower_ref, got_ref, *outs):
    half = upper_ref.shape[1]
    got = got_ref.at[:, :half, :], got_ref.at[:, half:, :]
    halve_kernel(after_ref, upper_ref, got[0], lower_ref, got[1], *outs)


def halve(after, *blocks):
    shape = (blocks[0].shape[0] // 2,) + blocks[0].shape[1:]
    return pl.pallas_call(
        halve_kernel if len(blocks) == 4 else first_halve_kernel,
        in_specs=[hbm] + [vmem] * len(blocks),
        out_specs=[vmem] * 4,
        out_shape=[pltpu.VMEM(shape, f32)] * 4,
        compiler_params=params(4),
        name="halve",
    )(after, *blocks)


def join_kernel(after_ref, upper_ref, upper_got_ref, lower_ref, lower_got_ref, out_hbm, out_ref, sems):
    del after_ref
    half = upper_ref.shape[1]
    copies = []
    for i in range(out_ref.shape[0]):
        out_ref[i, :half, :] = upper_ref[i] + upper_got_ref[i]
        out_ref[i, half:, :] = lower_ref[i] + lower_got_ref[i]
        copies.append(pltpu.make_async_copy(out_ref.at[i], out_hbm.at[i], sems.at[i]))
        copies[i].start()
    for copy in copies:
        copy.wait()


def finish_kernel(part_ref, basis_ref, out_ref):
    total = part_ref[0]
    for i in range(1, part_ref.shape[0]):
        total = total + part_ref[i]
    high, low = split(total * (1.0 / 32))
    b_high, b_low = split(basis_ref[...])
    rows = ((0,), (0,))
    wide = dot(high, jnp.concatenate([b_high, b_low], axis=1), rows)
    right = wide[:, :RANK] + wide[:, RANK:] + dot(low, b_high, rows)
    for i in range(out_ref.shape[0]):
        out_ref[i] = right[: out_ref.shape[1], :]


def update_kernel(slot, basis_ref, right_ref, sum_ref, *rest):
    out_hbm, right_hbm, basis_hbm, out_ref, sems = rest[3 * slot :]
    columns = sum_ref.shape[1]
    steps = columns // CHUNK
    m = lax.axis_index("core") ^ slot
    stores = [
        pltpu.make_async_copy(right_ref, right_hbm.at[m], sems.at[steps]),
        pltpu.make_async_copy(basis_ref, basis_hbm.at[m], sems.at[steps + 1]),
    ]
    for copy in stores:
        copy.start()
    high, low = split(basis_ref[...])
    wide = jnp.concatenate([high, low], axis=1)
    for j in range(steps):
        r_high, r_low = split(right_ref[cols(j), :])
        rebuilt = dot(wide, jnp.concatenate([r_high, r_high], axis=1), ((1,), (1,)))
        rebuilt = rebuilt + dot(high, r_low, ((1,), (1,)))
        out_ref[:, cols(j)] = sum_ref[:, cols(j)] - rebuilt
        copy = pltpu.make_async_copy(out_ref.at[:, cols(j)], out_hbm.at[m, :, cols(j)], sems.at[j])
        copy.start()
        stores.append(copy)
    for copy in stores:
        copy.wait()


def update(slot, basis, right, summed, previous=()):
    rows, columns = summed.shape
    return pl.pallas_call(
        functools.partial(update_kernel, slot),
        in_specs=[vmem] * 3 + [hbm] * len(previous),
        out_specs=[hbm] * 3,
        out_shape=[
            jax.ShapeDtypeStruct((2, rows, columns), f32),
            jax.ShapeDtypeStruct((2, columns, RANK), f32),
            jax.ShapeDtypeStruct((2, rows, RANK), f32),
        ],
        scratch_shapes=[
            pltpu.VMEM((rows, columns), f32),
            pltpu.SemaphoreType.DMA((2 + columns // CHUNK,)),
        ],
        input_output_aliases={3: 0, 4: 1, 5: 2} if previous else {},
        cost_estimate=pl.CostEstimate(
            flops=6 * rows * columns * RANK, bytes_accessed=8 * rows * columns, transcendentals=0
        ),
        compiler_params=params(8),
        name=("update_mine", "update_other")[slot],
    )(basis, right, summed, *previous)


def swap(x):
    return lax.ppermute(x, "core", [(0, 1), (1, 0)])


def cross(x, axis):
    return lax.ppermute(x, (axis + "h", axis + "l"), [(i, 3 - i) for i in range(4)])


def exchange(x, axes=PLANE):
    return lax.all_to_all(x, axes, 0, 0)


def on_device(gradients, feedback, seed_value):
    gradients = pltpu.with_memory_space_constraint(gradients[0], pltpu.HBM)
    feedback = pltpu.with_memory_space_constraint(feedback[0], pltpu.HBM)
    mats, rows, columns = gradients.shape
    depth = lax.axis_size("z")
    share = -(-rows // (CHIPS * TILE)) * TILE
    padded = CHIPS * share

    mine, other, upper, lower, tiles_other, summed, summed_other = pl.pallas_call(
        left_kernel,
        in_specs=[smem, hbm, hbm],
        out_specs=[vmem] * 5 + [hbm, vmem],
        out_shape=[pltpu.VMEM((padded, RANK), f32)] * 2
        + [pltpu.VMEM((CHIPS, rows // 2, LANES), f32)] * 2
        + [pltpu.VMEM((CHIPS, rows, LANES), f32)]
        + [pltpu.HBM((rows, columns), f32), pltpu.VMEM((rows, columns), f32)],
        scratch_shapes=[
            pltpu.VMEM((mats, rows, columns), bf16),
            pltpu.VMEM((mats, rows, columns), f32),
            pltpu.VMEM((columns, 2 * RANK), bf16),
            pltpu.SemaphoreType.DMA((columns // CHUNK, 4)),
        ],
        compiler_params=params(20),
        name="left_part",
    )(seed_value, gradients, feedback)

    left = mine + swap(other)
    left, tiles_other = lax.optimization_barrier((left, tiles_other))
    tiles_got = swap(tiles_other)
    left = exchange(left.reshape(CHIPS, share, RANK))
    upper, upper_send, lower, lower_send = halve(left, upper, lower, tiles_got)
    upper_got, lower_got = cross(upper_send, "x"), cross(lower_send, "y")
    left = exchange(sum_spread(left, depth), "z")
    upper, upper_send, lower, lower_send = halve(left, upper, upper_got, lower, lower_got)
    upper_got, lower_got = cross(upper_send, "y"), cross(lower_send, "x")
    left = exchange(sum_spread(left, CHIPS))

    quarter = pl.pallas_call(
        join_kernel,
        in_specs=[hbm] + [vmem] * 4,
        out_specs=hbm,
        out_shape=pltpu.HBM((CHIPS // 4, rows, LANES), f32),
        scratch_shapes=[pltpu.VMEM((CHIPS // 4, rows, LANES), f32), pltpu.SemaphoreType.DMA((CHIPS // 4,))],
        compiler_params=params(4),
        name="join",
    )(left, upper, upper_got, lower, lower_got)
    basis = pl.pallas_call(
        basis_kernel,
        in_specs=[vmem, hbm],
        out_specs=vmem,
        out_shape=pltpu.VMEM((rows, RANK), f32),
        cost_estimate=pl.CostEstimate(flops=5_000_000_000, bytes_accessed=400_000, transcendentals=0),
        compiler_params=params(8),
        name="basis",
    )(left.reshape(padded, RANK), quarter)
    basis_other = swap(basis)
    right = pl.pallas_call(
        finish_kernel,
        in_specs=[vmem, vmem],
        out_specs=vmem,
        out_shape=pltpu.VMEM((CHIPS, columns // CHIPS, RANK), f32),
        compiler_params=params(4),
        name="finish",
    )(exchange(quarter, ("xl", "yl")), basis)
    right = exchange(right).reshape(columns, RANK)
    right_other = swap(right)

    outs = update(0, basis, right, summed)
    new_feedback, right_factor, left_basis = update(1, basis_other, right_other, summed_other, outs)
    return new_feedback[None], left_basis, right_factor


def solution(mesh):
    fine = Mesh(mesh.devices.reshape(2, 2, 2, 2, 2, -1), PLANE + ("core", "z"))
    dp = PLANE + ("core",)
    placed = (P(dp, None, None, "z"), P(dp, None, None, "z"), P())
    return jax.shard_map(
        on_device,
        mesh=fine,
        in_specs=placed,
        out_specs=(P(dp, None, None, "z"), P(), P(None, "z", None)),
        check_vma=False,
    )
```
